256 devices in a mesh: ma: 64 (over x, z, core), freq: 4 (over y).
Axes of the slice: x: 4, y: 4, z: 8, core: 2. Of those that a mesh axis runs over, the one named last changes fastest.
Arguments:
- visibility: bfloat16 [2048, 2, 2, 1024], P('ma', None, None, 'freq'), may hold values from -6 to 6
- pair_baseline: int32 [4096, 1], replicated, may hold values from 0 to 1023
- beam_inverse: bfloat16 [256, 2, 2, 1024, 1024], P('ma', None, None, None, 'freq'), may hold values from -0.0625 to 0.0625
- block_rows: int32 [256], P('ma'), may hold values from 1 to 1024, as said below
- legendre: bfloat16 [256, 1024, 1024], P('ma', None, 'freq'), may hold values from -0.0078125 to 0.0078125
- circle_pixels: int32 [1024], P(('freq', 'ma')), may hold values from 4 to 2048, as said below
Outputs:
- sky_map: float32 [2, 1024, 2048], P(None, ('freq', 'ma'))
The draws below stay inside these ranges and needn't reach their ends.
Inputs may be any that keep to these rules, and one draw needn't show every extreme that they name: `pair_baseline`: every baseline is named by at least one feed pair. `block_rows`: 1024 is reached in every draw. `circle_pixels`: 2048 is reached in every draw.
All inputs are finite; a program needn't handle non-finite values.
Results may differ from the reference program's by a relative error of at most 0.006.
Values may be sent and summed in bfloat16 or wider, within the bound.
No kernel may reach another device: no remote copies, remote signals or barrier semaphores. Data moves between devices by JAX's collectives and lax.ppermute only.
A program may use at most 64 MiB of HBM per device.

```python
import math
import jax
import jax.numpy as jnp
from jax import lax

NB = 1024
NTIME = 2048
FREQ = 2
LPAD = 1024
NLAT = 1024
PMAX = 2048
PAIRS = 4096
MM = 256


def draw_block_rows(key, part):
    key = jax.random.fold_in(key, 11)
    mode_ids = jnp.arange(MM, dtype=jnp.int32)
    base = LPAD - mode_ids * (LPAD - LPAD // 8) // MM
    jitter = jax.random.randint(key, (MM,), 0, LPAD // 16 + 1, dtype=jnp.int32)
    return jnp.where(mode_ids == 0, LPAD, jnp.maximum(base - jitter, 1)).astype(jnp.int32)


def draw_circle_pixels(key, part):
    key = jax.random.fold_in(key, 23)
    circle_ids = jnp.arange(NLAT, dtype=jnp.int32)
    base = jnp.minimum(PMAX, jnp.minimum(4 * (circle_ids + 1), 4 * (NLAT - circle_ids)))
    jitter = jax.random.randint(key, (NLAT,), 0, 3, dtype=jnp.int32)
    return jnp.where(base < PMAX, jnp.maximum(4, base - 4 * jitter), PMAX).astype(jnp.int32)


def block_scale(rng, shape, shards, least, largest):
    factor_of, own = 1.0, jax.random.fold_in(rng, 6)
    for position, shards_of in shards:
        draws = jnp.exp(jax.random.uniform(jax.random.fold_in(own, position), (shards_of,), jnp.float32, least / len(shards), largest / len(shards)))
        factor_of = factor_of * jnp.repeat(draws, shape[position] // shards_of).reshape([-1 if axis == position else 1 for axis in range(len(shape))])
    return factor_of


def choose_distinct(rng, rows, number_of, top, lift):
    sequence = jax.random.permutation(jax.random.fold_in(rng, 1), number_of)
    pull = sequence
    for power in range(3):
        pull = pull * pull // number_of
    pull = pull * lift // number_of
    chance = jax.random.randint(jax.random.fold_in(rng, 2), (rows, number_of), 0, 4096) + pull
    holders = jax.random.permutation(jax.random.fold_in(rng, 3), rows)[jnp.arange(number_of) % rows]
    chance = jnp.where(jnp.arange(rows)[:, None] == holders[None, :], 1 << 14, chance)
    score = chance * number_of + jnp.arange(number_of)
    return lax.top_k(score.astype(jnp.int32), top)[1].astype(jnp.int32)


def bell_draw(own_key, dims, width, bound, cuts=(), kind=jnp.bfloat16):
    entries = width * jax.random.normal(own_key, dims, jnp.float32)
    if cuts:
        entries = entries * block_scale(own_key, dims, cuts, -0.22, 0.18)
    return jnp.clip(entries, -bound, bound).astype(kind)


def setup_inputs(seed: int = 0) -> dict:
    key_of = jax.random.split(jax.random.key(seed), 7)
    return {
        "visibility": bell_draw(key_of[0], (NTIME, 2, FREQ, NB), 1.0, 6.0, ((0, 64), (3, 4))),
        "pair_baseline": choose_distinct(key_of[1], PAIRS, NB, 1, 16),
        "beam_inverse": bell_draw(key_of[2], (MM, FREQ, 2, LPAD, NB), (2 * PAIRS) ** -0.5, 0.0625, ((0, 64), (4, 4))),
        "block_rows": draw_block_rows(jax.random.fold_in(key_of[6], 71), 0),
        "legendre": bell_draw(key_of[4], (MM, LPAD, NLAT), (2 * LPAD * MM) ** -0.5, 0.0078125, ((0, 64), (2, 4))),
        "circle_pixels": draw_circle_pixels(jax.random.fold_in(key_of[6], 71), 0),
    }


HIGH = lax.Precision.HIGH

def dft_tables(mode_ids, time_ids, length):
    phase = mode_ids[:, None] * time_ids[None, :] % length
    angle = phase.astype(jnp.float32) * (2.0 * math.pi / length)
    return (jnp.cos(angle), jnp.sin(angle))

def circle_tables(mode_ids, pixel_ids, count):
    phase = mode_ids * (2 * pixel_ids + 1) % (2 * count)
    angle = phase.astype(jnp.float32) * math.pi / count.astype(jnp.float32)
    factor = jnp.where(mode_ids == 0, 1.0, 2.0) * (pixel_ids < count)
    return (jnp.cos(angle) * factor, jnp.sin(angle) * factor)

def reference(visibility, pair_baseline, beam_inverse, block_rows, legendre, circle_pixels):
    ntime = visibility.shape[0]
    nfreq = visibility.shape[2]
    nbase = visibility.shape[3]
    modes = beam_inverse.shape[0]
    lrows = beam_inverse.shape[3]
    cosine, sine = dft_tables(jnp.arange(modes, dtype=jnp.int32), jnp.arange(ntime, dtype=jnp.int32), ntime)
    signal = visibility.astype(jnp.float32).reshape(ntime, 2, nfreq * nbase)
    real_in = signal[:, 0]
    imag_in = signal[:, 1]
    real_out = jnp.dot(cosine, real_in, precision=HIGH) + jnp.dot(sine, imag_in, precision=HIGH)
    imag_out = jnp.dot(cosine, imag_in, precision=HIGH) - jnp.dot(sine, real_in, precision=HIGH)
    spectrum = jnp.stack([real_out, imag_out], 1).reshape(modes, 2, nfreq, nbase) * (1.0 / math.sqrt(ntime))
    counts = lax.optimization_barrier(jnp.sum((pair_baseline == jnp.arange(nbase, dtype=jnp.int32)[None, :]).astype(jnp.float32), 0))
    weighted = (spectrum * jnp.sqrt(counts)).astype(jnp.bfloat16)

    def project(inputs):
        beam_block, vis_block = inputs
        product = jnp.einsum('fclb,dfb->fcdl', beam_block.astype(jnp.float32), vis_block.astype(jnp.float32))
        real_part = product[:, 0, 0] - product[:, 1, 1]
        imag_part = product[:, 0, 1] + product[:, 1, 0]
        return jnp.stack([real_part, imag_part], 1)
    harmonics = lax.map(project, (beam_inverse, weighted))
    live = jnp.arange(lrows, dtype=jnp.int32)[None, :] < block_rows[:, None]
    harmonics = jnp.where(live[:, None, None, :], harmonics, 0.0).astype(jnp.bfloat16)

    def legendre_sum(inputs):
        harm_block, table_block = inputs
        return jnp.einsum('fdl,lr->fdr', harm_block.astype(jnp.float32), table_block.astype(jnp.float32))
    latitude = lax.map(legendre_sum, (harmonics, legendre)).astype(jnp.bfloat16)
    mode_ids = jnp.arange(modes, dtype=jnp.int32)[:, None]
    pixel_ids = jnp.arange(PMAX, dtype=jnp.int32)[None, :]

    def circle_map(inputs):
        column, count = inputs
        cos_table, sin_table = circle_tables(mode_ids, pixel_ids, count)
        values = column.astype(jnp.float32)
        return jnp.dot(values[:, :, 0].T, cos_table, precision=HIGH) - jnp.dot(values[:, :, 1].T, sin_table, precision=HIGH)
    circles = lax.map(circle_map, (jnp.moveaxis(latitude, 3, 0), circle_pixels))
    return jnp.moveaxis(circles, 0, 1)
```

```python
import math

import jax
import jax.numpy as jnp
import ml_dtypes
import numpy as np
from jax import lax
from jax.experimental import pallas as pl
from jax.experimental.pallas import tpu as pltpu
from jax.sharding import PartitionSpec as P

PMAX = 2048
INNER = 128
OUTER = PMAX // INNER
COS = (
    1.0, -19.739208221435547, 64.93939208984375, -85.45664978027344,
    60.24201202392578, -26.403913497924805, 7.797765254974365, -1.4502166509628296,
)
SIN = (
    6.2831854820251465, -41.34170150756836, 81.6052474975586, -76.70579528808594,
    42.057708740234375, -15.086281776428223, 3.7804296016693115, -0.6196905970573425,
)


def split_np(table):
    high = table.astype(ml_dtypes.bfloat16)
    low = (table - high.astype(np.float64)).astype(ml_dtypes.bfloat16)
    return high, low


def dft_constant(modes, length):
    phase = np.arange(modes)[:, None] * np.arange(length)[None, :] % length
    angle = phase * (2.0 * math.pi / length)
    table = np.concatenate([np.cos(angle), np.sin(angle)], 0) / math.sqrt(length)
    return np.concatenate(split_np(table), 0)


def split(x):
    high = x.astype(jnp.bfloat16)
    return high, (x - high.astype(jnp.float32)).astype(jnp.bfloat16)


def cos_sin(phase, period, inverse):
    rest = phase - jnp.round(phase * inverse) * period
    turn = rest * inverse
    square = turn * turn
    cosine = jnp.full_like(square, COS[-1])
    sine = jnp.full_like(square, SIN[-1])
    for c, s in zip(COS[-2::-1], SIN[-2::-1]):
        cosine = cosine * square + c
        sine = sine * square + s
    return cosine, sine * turn


def mode_of_lane(shape, modes, mode_dev):
    lane = lax.broadcasted_iota(jnp.int32, shape, len(shape) - 1)
    blocks = modes // mode_dev
    return lane % blocks * mode_dev + lane // blocks


def table_kernel(modes, mode_dev, count_ref, outer_ref, inner_ref):
    for circle in range(count_ref.shape[0]):
        count = count_ref[circle].astype(jnp.float32)
        period = jnp.full((1, modes), 2.0 * count, jnp.float32)
        inverse = 1.0 / period
        mode = mode_of_lane((OUTER, modes), modes, mode_dev)
        step = lax.broadcasted_iota(jnp.int32, (OUTER, modes), 0) * (2 * INNER)
        cosine, sine = cos_sin((mode * step).astype(jnp.float32), period, inverse)
        outer_ref[circle, 0] = cosine
        outer_ref[circle, 1] = sine
        mode = mode_of_lane((INNER, modes), modes, mode_dev)
        step = lax.broadcasted_iota(jnp.int32, (INNER, modes), 0) * 2 + 1
        cosine, sine = cos_sin((mode * step).astype(jnp.float32), period, inverse)
        factor = jnp.where(mode == 0, 1.0, 2.0)
        for part, value in enumerate((cosine * factor, -sine * factor)):
            high, low = split(value)
            columns = pl.ds(part * modes, modes)
            inner_ref[circle, 0, :, columns] = high
            inner_ref[circle, 1, :, columns] = low


def synthesis_kernel(count_ref, value_ref, outer_ref, inner_ref, map_ref):
    circles = outer_ref.shape[0]
    nfreq = map_ref.shape[0]
    for circle in range(circles):
        rows = []
        cosine = outer_ref[circle, 0]
        sine = outer_ref[circle, 1]
        for f in range(nfreq):
            row = (circle * nfreq + f) * 2
            real = value_ref[row : row + 1, :]
            imag = value_ref[row + 1 : row + 2, :]
            rows.append(
                jnp.concatenate([real * cosine - imag * sine, real * sine + imag * cosine], 1)
            )
        high, low = split(jnp.concatenate(rows, 0))
        dims = (((1,), (1,)), ((), ()))
        dot = lambda a, b: lax.dot_general(a, b, dims, preferred_element_type=jnp.float32)
        result = dot(high, inner_ref[circle, 0])
        result += dot(low, inner_ref[circle, 0]) + dot(high, inner_ref[circle, 1])
        pixel = lax.broadcasted_iota(jnp.int32, (OUTER, INNER), 0) * INNER
        pixel += lax.broadcasted_iota(jnp.int32, (OUTER, INNER), 1)
        keep = pixel < count_ref[circle]
        for f in range(nfreq):
            part = jnp.where(keep, result[f * OUTER : (f + 1) * OUTER], 0.0)
            for q in range(OUTER):
                map_ref[f, circle : circle + 1, q * INNER : (q + 1) * INNER] = part[q : q + 1]


def body(visibility, pair_baseline, beam_inverse, block_rows, legendre, circle_pixels):
    ma_count = lax.axis_size("ma")
    freq_count = lax.axis_size("freq")
    ma_place = lax.axis_index("ma")
    freq_place = lax.axis_index("freq")
    time_dev, _, nfreq, base_dev = visibility.shape
    ntime = time_dev * ma_count
    mode_dev = beam_inverse.shape[0]
    lrows = beam_inverse.shape[3]
    modes = mode_dev * ma_count
    nbase = base_dev * freq_count
    circles = circle_pixels.shape[0]
    base_piece = base_dev // ma_count
    columns = 2 * nfreq * base_piece

    moved = lax.all_to_all(
        visibility.reshape(time_dev, 2, nfreq, ma_count, base_piece)
        .transpose(3, 0, 1, 2, 4)
        .reshape(ma_count, time_dev * columns // 128, 128),
        "ma", 0, 0,
    )
    smem = pl.BlockSpec(memory_space=pltpu.SMEM)
    vmem = pl.BlockSpec(memory_space=pltpu.VMEM)
    outer, inner = pl.pallas_call(
        lambda *refs: table_kernel(modes, mode_dev, *refs),
        out_shape=(
            jax.ShapeDtypeStruct((circles, 2, OUTER, modes), jnp.float32),
            jax.ShapeDtypeStruct((circles, 2, INNER, 2 * modes), jnp.bfloat16),
        ),
        in_specs=[smem],
        out_specs=(vmem, vmem),
        cost_estimate=pl.CostEstimate(flops=10000000, bytes_accessed=1200000, transcendentals=0),
    )(circle_pixels)
    counts = jnp.sum(
        (pair_baseline == jnp.arange(nbase, dtype=jnp.int32)[None, :]).astype(jnp.float32), 0
    )
    weight_piece = lax.dynamic_slice_in_dim(
        jnp.sqrt(counts), freq_place * base_dev + ma_place * base_piece, base_piece, 0
    )
    signal = moved.reshape(ntime, columns)
    table = jnp.asarray(dft_constant(modes, ntime))
    sums = jnp.dot(table, signal, preferred_element_type=jnp.float32)
    sums = sums.reshape(2, 2, modes, 2, nfreq, base_piece).sum(0)
    real = sums[0, :, 0] + sums[1, :, 1]
    imag = sums[0, :, 1] - sums[1, :, 0]
    spectrum = (jnp.stack([real, imag], 1) * weight_piece).astype(jnp.bfloat16)
    weighted = lax.all_to_all(
        spectrum.reshape(ma_count, 1, mode_dev * columns), "ma", 0, 0
    )
    weighted = weighted.reshape(ma_count, mode_dev, 2, nfreq, base_piece)
    weighted = weighted.transpose(1, 2, 3, 0, 4).reshape(mode_dev, 2, nfreq, base_dev)

    product = jnp.einsum(
        "mfclb,mdfb->mfcdl", beam_inverse, weighted, preferred_element_type=jnp.float32
    )
    real_part = product[:, :, 0, 0] - product[:, :, 1, 1]
    imag_part = product[:, :, 0, 1] + product[:, :, 1, 0]
    partial_value = jnp.stack([real_part, imag_part], 2)
    harmonics = lax.psum(partial_value, "freq")
    live = jnp.arange(lrows, dtype=jnp.int32)[None, :] < block_rows[:, None]
    harmonics = jnp.where(live[:, None, None, :], harmonics, 0.0).astype(jnp.bfloat16)
    latitude = jnp.einsum(
        "mfdl,mlr->mfdr", harmonics, legendre, preferred_element_type=jnp.float32
    ).astype(jnp.bfloat16)

    latitude = latitude.reshape(mode_dev, nfreq, 2, ma_count, circles)
    regrouped = lax.all_to_all(
        latitude.transpose(3, 0, 4, 1, 2).reshape(ma_count, 1, mode_dev * circles * nfreq * 2),
        "ma", 0, 0,
    )
    values = regrouped.reshape(ma_count, mode_dev, circles * nfreq * 2).transpose(2, 1, 0)
    values = values.reshape(circles * nfreq * 2, modes).astype(jnp.float32)
    return pl.pallas_call(
        synthesis_kernel,
        out_shape=jax.ShapeDtypeStruct((nfreq, circles, PMAX), jnp.float32),
        in_specs=[smem, vmem, vmem, vmem],
        out_specs=vmem,
    )(circle_pixels, values, outer, inner)


def solution(mesh):
    return jax.shard_map(
        body,
        mesh=mesh,
        in_specs=(
            P("ma", None, None, "freq"),
            P(),
            P("ma", None, None, None, "freq"),
            P("ma"),
            P("ma", None, "freq"),
            P(("freq", "ma")),
        ),
        out_specs=P(None, ("freq", "ma"), None),
        check_vma=False,
    )
```

```python
import math

import jax
import jax.numpy as jnp
from jax import lax
from jax.experimental import pallas as pl
from jax.experimental.pallas import tpu as pltpu
from jax.sharding import PartitionSpec as P

PMAX = 2048
INNER = 128
OUTER = PMAX // INNER
COS = (
    1.0, -19.739208221435547, 64.93939208984375, -85.45664978027344,
    60.24201202392578, -26.403913497924805, 7.797765254974365, -1.4502166509628296,
)
SIN = (
    6.2831854820251465, -41.34170150756836, 81.6052474975586, -76.70579528808594,
    42.057708740234375, -15.086281776428223, 3.7804296016693115, -0.6196905970573425,
)
BF16 = jnp.bfloat16
F32 = jnp.float32
SMEM = pl.BlockSpec(memory_space=pltpu.SMEM)
VMEM = pl.BlockSpec(memory_space=pltpu.VMEM)


def split(x):
    high = x.astype(BF16)
    return high, (x - high.astype(F32)).astype(BF16)


def iota(shape, dimension):
    return lax.broadcasted_iota(jnp.int32, shape, dimension)


def polynomial(square, terms):
    total = jnp.full_like(square, terms[-1])
    for term in terms[-2::-1]:
        total = total * square + term
    return total


def cos_sin(phase, period, inverse):
    rest = phase - jnp.round(phase * inverse) * period
    turn = rest * inverse
    square = turn * turn
    return polynomial(square, COS), polynomial(square, SIN) * turn


def dot(a, b, contract):
    return lax.dot_general(a, b, ((contract[:1], contract[1:]), ((), ())), preferred_element_type=F32)


def call(kernel, outs, specs, *args, cost=None, name=None):
    args = [
        pltpu.with_memory_space_constraint(a, pltpu.VMEM) if s is VMEM else a
        for a, s in zip(args, specs)
    ]
    flops, size = cost or (1000000, 100000)
    return pl.pallas_call(
        kernel,
        out_shape=tuple(pltpu.VMEM(s, d) for s, d in outs),
        in_specs=list(specs),
        out_specs=tuple(VMEM for _ in outs),
        cost_estimate=pl.CostEstimate(flops=flops, bytes_accessed=size, transcendentals=0),
        compiler_params=pltpu.CompilerParams(vmem_limit_bytes=30 * 1024 * 1024),
        name=name,
    )(*args)


def phase_kernel(time_dev, nfreq, ntime, place_ref, table_ref):
    rows, width = table_ref.shape[1:]
    row = iota((rows, 1), 0)
    column = iota((1, width), 1)
    mode, part_out, freq_out = row // (2 * nfreq), row // nfreq % 2, row % nfreq
    source = jnp.where(column < width // 2, place_ref[0], place_ref[1])
    inside = column % (width // 2)
    time = source * time_dev + inside // (2 * nfreq)
    part_in, freq_in = inside // nfreq % 2, inside % nfreq
    phase = mode * time + (part_out - part_in) * (ntime // 4)
    turn = ((phase + ntime // 2) % ntime - ntime // 2).astype(F32) * (1.0 / ntime)
    value = polynomial(turn * turn, COS) * (1.0 / math.sqrt(ntime))
    value = jnp.where(freq_out == freq_in, value, 0.0)
    table_ref[0], table_ref[1] = split(value)


def time_kernel(table_ref, own_ref, other_ref, out_ref):
    signal = jnp.concatenate([own_ref[...], other_ref[...]], 0)
    total = dot(table_ref[0], signal, (1, 0)) + dot(table_ref[1], signal, (1, 0))
    out_ref[...] = total.reshape(out_ref.shape).astype(BF16)


def beam_kernel(nfreq, part_ref, weight_ref, beam_ref, total_ref, send_ref):
    sources, rows, width = part_ref.shape
    cores = sources // 2
    sums = part_ref[...].astype(F32).reshape(cores, 2, rows, width).sum(0)
    weighted = jnp.concatenate([sums[0], sums[1]], 1) * weight_ref[...]
    row = iota(weighted.shape, 0)
    turned = jnp.where(
        row // nfreq % 2 == 0,
        -pltpu.roll(weighted, rows - nfreq, 0),
        pltpu.roll(weighted, nfreq, 0),
    )
    total = jnp.zeros(total_ref.shape, F32)
    for m in range(beam_ref.shape[0]):
        for f in range(nfreq):
            live = (row // (2 * nfreq) == m) & (row % nfreq == f)
            for c, value in enumerate((weighted, turned)):
                left = jnp.where(live, value, 0.0).astype(BF16)
                total += dot(left, beam_ref[m, f, c], (1, 1))
    total_ref[...] = total
    send_ref[...] = total.astype(BF16)


def legendre_kernel(
    rows_ref, own_ref, first_ref, second_ref, third_ref, table_ref, out_ref, scratch_ref
):
    total = own_ref[...] + first_ref[...].astype(F32)
    total = total + second_ref[...].astype(F32) + third_ref[...].astype(F32)
    modes = table_ref.shape[0]
    each = total.shape[0] // modes
    row = iota(total.shape, 0)
    column = iota(total.shape, 1)
    latitude = jnp.zeros((total.shape[0], table_ref.shape[2]), F32)
    for m in range(modes):
        live = (row // each == m) & (column < rows_ref[m])
        latitude += dot(jnp.where(live, total, 0.0).astype(BF16), table_ref[m], (1, 0))
    scratch_ref[...] = latitude.astype(BF16).astype(F32).T
    dests, _, width = out_ref.shape
    circles = scratch_ref.shape[0] // dests
    pieces = [scratch_ref[pl.ds(j, dests, circles), :] for j in range(circles)]
    out_ref[...] = jnp.concatenate(pieces, 1).reshape(out_ref.shape)


def mode_of(position, modes, mode_dev):
    blocks = modes // mode_dev
    return position % blocks * mode_dev + position // blocks


def table_kernel(modes, mode_dev, count_ref, outer_ref, inner_ref):
    for circle in range(count_ref.shape[0]):
        period = jnp.full((1, 1), 2 * count_ref[circle], jnp.int32).astype(F32)
        inverse = 1.0 / period
        mode = mode_of(iota((OUTER, modes), 1), modes, mode_dev)
        step = iota((OUTER, modes), 0) * (2 * INNER)
        outer_ref[circle, 0], outer_ref[circle, 1] = cos_sin(
            (mode * step).astype(F32), period, inverse
        )
        mode = mode_of(iota((modes, INNER), 0), modes, mode_dev)
        step = iota((modes, INNER), 1) * 2 + 1
        cosine, sine = cos_sin((mode * step).astype(F32), period, inverse)
        factor = jnp.where(mode == 0, 1.0, 2.0)
        for part, value in enumerate((cosine * factor, -sine * factor)):
            high, low = split(value)
            inner_ref[circle, part * modes : (part + 1) * modes, :INNER] = high
            inner_ref[circle, part * modes : (part + 1) * modes, INNER:] = low


def synthesis_kernel(nfreq, count_ref, value_ref, outer_ref, inner_ref, map_ref):
    circles = outer_ref.shape[0]
    sources, _, width = value_ref.shape
    values = value_ref[...].reshape(sources, width).T
    each = width // circles
    wide = 2 * nfreq
    results = []
    for circle in range(circles):
        block = values[circle * each : (circle + 1) * each]
        block = jnp.concatenate([block[i : i + wide] for i in range(0, each, wide)], 1)
        cosine = outer_ref[circle, 0]
        sine = outer_ref[circle, 1]
        rows = []
        for f in range(nfreq):
            real = block[f : f + 1]
            imag = block[nfreq + f : nfreq + f + 1]
            rows.append(
                jnp.concatenate([real * cosine - imag * sine, real * sine + imag * cosine], 1)
            )
        high, low = split(jnp.concatenate(rows, 0))
        result = dot(jnp.concatenate([high, low], 0), inner_ref[circle], (1, 0))
        half = nfreq * OUTER
        results.append(
            result[:half, :INNER] + (result[:half, INNER:] + result[half:, :INNER])
        )
    pixel = iota((OUTER, INNER), 0) * INNER + iota((OUTER, INNER), 1)
    for circle in range(circles):
        keep = pixel < count_ref[circle]
        for f in range(nfreq):
            part = jnp.where(keep, results[circle][f * OUTER : (f + 1) * OUTER], 0.0)
            for q in range(OUTER):
                map_ref[f, circle : circle + 1, q * INNER : (q + 1) * INNER] = part[q : q + 1]


def body(visibility, pair_baseline, beam_inverse, block_rows, legendre, circle_pixels):
    ma_count = lax.axis_size("ma")
    freq_count = lax.axis_size("freq")
    ma_place = lax.axis_index("ma")
    freq_place = lax.axis_index("freq")
    time_dev, _, nfreq, base_dev = visibility.shape
    ntime = time_dev * ma_count
    mode_dev, _, _, lrows, _ = beam_inverse.shape
    modes = mode_dev * ma_count
    circles = circle_pixels.shape[0]
    base_half = base_dev // 2
    core = ma_place % 2
    rows = mode_dev * 2 * nfreq

    def half(which):
        piece = lax.dynamic_slice_in_dim(visibility, which * base_half, base_half, 3)
        return piece.reshape(time_dev * 2 * nfreq, base_half)

    other = lax.ppermute(half(1 - core), "ma", [(i, i ^ 1) for i in range(ma_count)])
    place = jnp.stack([ma_place, ma_place + 1 - 2 * core]).astype(jnp.int32)
    (table,) = call(
        lambda *refs: phase_kernel(time_dev, nfreq, ntime, *refs),
        [((2, modes * 2 * nfreq, 4 * time_dev * nfreq), BF16)],
        [SMEM],
        place,
        cost=(5000000, 1000000), name="phases",
    )
    (partial_spectrum,) = call(
        time_kernel,
        [((ma_count, rows, base_half), BF16)],
        [VMEM, VMEM, VMEM],
        table, half(core), other, name="time_sum",
    )
    received = lax.all_to_all(partial_spectrum, "ma", 0, 0)

    outer, inner = call(
        lambda *refs: table_kernel(modes, mode_dev, *refs),
        [((circles, 2, OUTER, modes), F32), ((circles, 2 * modes, 2 * INNER), BF16)],
        [SMEM],
        circle_pixels,
        cost=(10000000, 1200000), name="circle_tables",
    )
    base_ids = freq_place * base_dev + jnp.arange(base_dev, dtype=jnp.int32)
    weight = jnp.sqrt(jnp.sum((pair_baseline == base_ids[None, :]).astype(F32), 0))[None, :]

    own, send = call(
        lambda *refs: beam_kernel(nfreq, *refs),
        [((rows, lrows), F32), ((rows, lrows), BF16)],
        [VMEM, VMEM, VMEM],
        received, weight, beam_inverse,
        cost=(300000000, 17000000), name="beam",
    )
    arrived = [
        lax.ppermute(send, "freq", [(i, (i + k) % freq_count) for i in range(freq_count)])
        for k in range(1, freq_count)
    ]
    latitude = pl.pallas_call(
        legendre_kernel,
        out_shape=(pltpu.VMEM((ma_count, 1, circles * rows), F32),),
        in_specs=[SMEM] + [VMEM] * 5,
        out_specs=(VMEM,),
        scratch_shapes=[pltpu.VMEM((legendre.shape[2], rows), F32)],
        name="legendre",
    )(
        block_rows,
        *(
            pltpu.with_memory_space_constraint(a, pltpu.VMEM)
            for a in (own, *arrived, legendre)
        ),
    )[0]
    regrouped = lax.all_to_all(latitude, "ma", 0, 0)
    return pl.pallas_call(
        lambda *refs: synthesis_kernel(nfreq, *refs),
        out_shape=jax.ShapeDtypeStruct((nfreq, circles, PMAX), F32),
        in_specs=[SMEM, VMEM, VMEM, VMEM],
        out_specs=VMEM,
        name="synthesis",
    )(
        circle_pixels,
        *(pltpu.with_memory_space_constraint(a, pltpu.VMEM) for a in (regrouped, outer, inner)),
    )


def solution(mesh):
    return jax.shard_map(
        body,
        mesh=mesh,
        in_specs=(
            P("ma", None, None, "freq"),
            P(),
            P("ma", None, None, None, "freq"),
            P("ma"),
            P("ma", None, "freq"),
            P(("freq", "ma")),
        ),
        out_specs=P(None, ("freq", "ma"), None),
        check_vma=False,
    )
```

```python
import math

import jax
import jax.numpy as jnp
import ml_dtypes
import numpy as np
from jax import lax
from jax.experimental import pallas as pl
from jax.experimental.pallas import tpu as pltpu
from jax.sharding import PartitionSpec as P

PMAX = 2048
INNER = 128
OUTER = PMAX // INNER
NEAR = 3
COS = (
    1.0, -19.739208221435547, 64.93939208984375, -85.45664978027344,
    60.24201202392578, -26.403913497924805, 7.797765254974365, -1.4502166509628296,
)
SIN = (
    6.2831854820251465, -41.34170150756836, 81.6052474975586, -76.70579528808594,
    42.057708740234375, -15.086281776428223, 3.7804296016693115, -0.6196905970573425,
)
BF16 = jnp.bfloat16
F32 = jnp.float32
SMEM = pl.BlockSpec(memory_space=pltpu.SMEM)
VMEM = pl.BlockSpec(memory_space=pltpu.VMEM)
ANY = pl.BlockSpec(memory_space=pl.ANY)
PARAMS = pltpu.CompilerParams(vmem_limit_bytes=16 * 1024 * 1024)


def split(x):
    high = x.astype(BF16)
    return high, (x - high.astype(F32)).astype(BF16)


def iota(shape, dimension):
    return lax.broadcasted_iota(jnp.int32, shape, dimension)


def polynomial(square, terms):
    total = jnp.full_like(square, terms[-1])
    for term in terms[-2::-1]:
        total = total * square + term
    return total


def cos_sin(phase, period, inverse):
    rest = phase - jnp.round(phase * inverse) * period
    turn = rest * inverse
    square = turn * turn
    return polynomial(square, COS), polynomial(square, SIN) * turn


def dot(a, b, contract):
    return lax.dot_general(a, b, ((contract[:1], contract[1:]), ((), ())), preferred_element_type=F32)


def call(kernel, outs, specs, *args, name=None):
    args = [
        pltpu.with_memory_space_constraint(a, pltpu.VMEM) if s is VMEM else a
        for a, s in zip(args, specs)
    ]
    return pl.pallas_call(
        kernel,
        out_shape=tuple(pltpu.VMEM(s, d) for s, d in outs),
        in_specs=list(specs),
        out_specs=tuple(VMEM for _ in outs),
        compiler_params=PARAMS,
        name=name,
    )(*args)


def phase_table(modes, nfreq, chip_times, ntime):
    row = np.arange(2 * modes * nfreq)[:, None]
    column = np.arange(chip_times * 2 * nfreq)[None, :]
    part_out, mode, freq_out = row // (modes * nfreq), row // nfreq % modes, row % nfreq
    time, part_in, freq_in = column // (2 * nfreq), column // nfreq % 2, column % nfreq
    phase = (mode * time + (part_out - part_in) * (ntime // 4)) % ntime
    value = np.cos(phase * (2.0 * math.pi / ntime)) / math.sqrt(ntime) * (freq_out == freq_in)
    high = value.astype(ml_dtypes.bfloat16)
    low = (value - high.astype(np.float64)).astype(ml_dtypes.bfloat16)
    return np.stack([high, low])


def fetch_kernel(place_ref, table_ref, signal_ref, near_ref, own_ref, semaphores):
    width = own_ref.shape[3]
    start = pl.multiple_of(place_ref[0] % 2 * width, width)
    copies = [
        pltpu.make_async_copy(
            signal_ref.at[:, :, :, pl.ds(start, width)], own_ref, semaphores.at[0]
        ),
        pltpu.make_async_copy(table_ref, near_ref, semaphores.at[1]),
    ]
    for copy in copies:
        copy.start()
    for copy in copies:
        copy.wait()


def time_kernel(nfreq, chips, place_ref, table_ref, own_ref, other_ref, out_ref):
    even = place_ref[0] % 2 == 0
    own, other = own_ref[...], other_ref[...]
    signal = jnp.concatenate([jnp.where(even, own, other), jnp.where(even, other, own)], 0)
    total = dot(table_ref[0], signal, (1, 0)) + dot(table_ref[1], signal, (1, 0))
    sources, rows, width = out_ref.shape
    phase = iota((chips * nfreq, width), 0) // nfreq * (place_ref[0] // 2)
    turn = ((phase + chips // 2) % chips - chips // 2).astype(F32) * (1.0 / chips)
    square = turn * turn
    cosine, sine = polynomial(square, COS)[None], (polynomial(square, SIN) * turn)[None]
    real, imag = total.reshape(2, -1, chips * nfreq, width)
    shape = (sources, rows // 2, width)
    real, imag = real * cosine + imag * sine, imag * cosine - real * sine
    out_ref[...] = jnp.concatenate([real.reshape(shape), imag.reshape(shape)], 1).astype(BF16)


def side_kernel(nfreq, first_ref, pair_ref, beam_ref, weight_ref, *refs):
    *block_refs, semaphores = refs
    copies = fetch_blocks(nfreq, beam_ref, 0, block_refs, semaphores)
    shape = (weight_ref.shape[1], pair_ref.shape[1])
    ids = iota(shape, 0) + first_ref[0]
    total = jnp.zeros(shape, F32)
    for i in range(pair_ref.shape[0]):
        total += jnp.where(pair_ref[i : i + 1, :] == ids, 1.0, 0.0)
    weight_ref[...] = jnp.sqrt(jnp.sum(total.T, 0, keepdims=True))
    for copy in copies:
        copy.wait()


def fetch_blocks(nfreq, beam_ref, first, block_refs, semaphores):
    copies = [
        pltpu.make_async_copy(
            beam_ref.at[(first + i) // nfreq, (first + i) % nfreq], block_ref, semaphores.at[i]
        )
        for i, block_ref in enumerate(block_refs)
    ]
    for copy in copies:
        copy.start()
    return copies


def beam_kernel(nfreq, part_ref, weight_ref, beam_ref, *refs):
    *near_refs, total_ref, send_ref, far_ref, semaphores = refs
    near = len(near_refs)
    far_refs = [far_ref.at[i] for i in range(far_ref.shape[0])]
    copies = fetch_blocks(nfreq, beam_ref, near, far_refs, semaphores)
    sources, rows, width = part_ref.shape
    half = rows // 2
    sums = part_ref[...].astype(F32).reshape(sources // 2, 2, rows, width).sum(0)
    weighted = jnp.concatenate([sums[0], sums[1]], 1) * weight_ref[...]
    turned = jnp.concatenate([-weighted[half:], weighted[:half]], 0)
    row = iota((2 * rows, weighted.shape[1]), 0) % half
    lefts = [jnp.concatenate(split(value), 0) for value in (weighted, turned)]
    total = jnp.zeros((2 * rows, total_ref.shape[1]), F32)
    for i, block_ref in enumerate([*near_refs, *far_refs]):
        if i >= near:
            copies[i - near].wait()
        for c in range(2):
            left = jnp.where(row == i, lefts[c], jnp.zeros_like(lefts[c]))
            total += dot(left, block_ref[c], (1, 1))
    total = total[:rows] + total[rows:]
    total_ref[...] = total
    send_ref[...] = total.astype(BF16)


def legendre_fetch_kernel(after_ref, table_ref, near_ref, semaphore):
    del after_ref
    copy = pltpu.make_async_copy(table_ref, near_ref, semaphore)
    copy.start()
    copy.wait()


def legendre_kernel(
    nfreq, rows_ref, own_ref, first_ref, second_ref, third_ref, table_ref, out_ref, scratch_ref
):
    total = own_ref[...] + first_ref[...].astype(F32)
    total = total + second_ref[...].astype(F32) + third_ref[...].astype(F32)
    rows = total.shape[0]
    left = jnp.concatenate(split(total), 0)
    row = iota(left.shape, 0) // nfreq
    column = iota(left.shape, 1)
    modes = table_ref.shape[0]
    latitude = jnp.zeros((2 * rows, table_ref.shape[2]), F32)
    for m in range(modes):
        live = (row % modes == m) & (column < rows_ref[m])
        latitude += dot(jnp.where(live, left, jnp.zeros_like(left)), table_ref[m], (1, 0))
    scratch_ref[...] = (latitude[:rows] + latitude[rows:]).T
    dests, _, width = out_ref.shape
    circles = scratch_ref.shape[0] // dests
    pieces = [scratch_ref[pl.ds(j, dests, circles), :] for j in range(circles)]
    out_ref[...] = jnp.concatenate(pieces, 1).reshape(out_ref.shape)


def mode_of(position, modes, mode_dev):
    blocks = modes // mode_dev
    return position % blocks * mode_dev + position // blocks


def table_kernel(modes, mode_dev, count_ref, outer_ref, inner_ref):
    for circle in range(count_ref.shape[0]):
        period = jnp.full((1, 1), 2 * count_ref[circle], jnp.int32).astype(F32)
        inverse = 1.0 / period
        mode = mode_of(iota((OUTER, modes), 1), modes, mode_dev)
        step = iota((OUTER, modes), 0) * (2 * INNER)
        outer_ref[circle, 0], outer_ref[circle, 1] = cos_sin(
            (mode * step).astype(F32), period, inverse
        )
        mode = mode_of(iota((modes, INNER), 0), modes, mode_dev)
        step = iota((modes, INNER), 1) * 2 + 1
        cosine, sine = cos_sin((mode * step).astype(F32), period, inverse)
        factor = jnp.where(mode == 0, 1.0, 2.0)
        for part, value in enumerate((cosine * factor, -sine * factor)):
            high, low = split(value)
            inner_ref[circle, part * modes : (part + 1) * modes, :INNER] = high
            inner_ref[circle, part * modes : (part + 1) * modes, INNER:] = low


def synthesis_kernel(nfreq, count_ref, value_ref, outer_ref, inner_ref, map_ref):
    circles = outer_ref.shape[0]
    sources, _, width = value_ref.shape
    values = value_ref[...].reshape(sources, width).T
    each = width // circles
    results = []
    for circle in range(circles):
        cosine = outer_ref[circle, 0]
        sine = outer_ref[circle, 1]
        rows = []
        for f in range(nfreq):
            start = circle * each + f
            real, imag = (
                jnp.concatenate([values[i : i + 1] for i in range(at, at + each // 2, nfreq)], 1)
                for at in (start, start + each // 2)
            )
            rows.append(
                jnp.concatenate([real * cosine - imag * sine, real * sine + imag * cosine], 1)
            )
        high, low = split(jnp.concatenate(rows, 0))
        result = dot(jnp.concatenate([high, low], 0), inner_ref[circle], (1, 0))
        half = nfreq * OUTER
        results.append(
            result[:half, :INNER] + (result[:half, INNER:] + result[half:, :INNER])
        )
    pixel = iota((OUTER, INNER), 0) * INNER + iota((OUTER, INNER), 1)
    for circle in range(circles):
        keep = pixel < count_ref[circle]
        for f in range(nfreq):
            part = jnp.where(keep, results[circle][f * OUTER : (f + 1) * OUTER], 0.0)
            for q in range(OUTER):
                map_ref[f, circle : circle + 1, q * INNER : (q + 1) * INNER] = part[q : q + 1]


def body(visibility, pair_baseline, beam_inverse, block_rows, legendre, circle_pixels):
    ma_count = lax.axis_size("ma")
    freq_count = lax.axis_size("freq")
    ma_place = lax.axis_index("ma")
    freq_place = lax.axis_index("freq")
    time_dev, _, nfreq, base_dev = visibility.shape
    ntime = time_dev * ma_count
    mode_dev, _, _, lrows, _ = beam_inverse.shape
    modes = mode_dev * ma_count
    circles = circle_pixels.shape[0]
    base_half = base_dev // 2
    rows = mode_dev * 2 * nfreq

    other = lax.ppermute(visibility, "ma", [(i, i ^ 1) for i in range(ma_count)])
    other = lax.dynamic_slice_in_dim(other, ma_place % 2 * base_half, base_half, 3)
    table = jnp.asarray(phase_table(modes, nfreq, 2 * time_dev, ntime))
    near, own = pl.pallas_call(
        fetch_kernel,
        out_shape=(pltpu.VMEM(table.shape, BF16), pltpu.VMEM(other.shape, BF16)),
        in_specs=[SMEM, ANY, ANY],
        out_specs=(VMEM, VMEM),
        scratch_shapes=[pltpu.SemaphoreType.DMA((2,))],
        compiler_params=PARAMS,
        cost_estimate=pl.CostEstimate(flops=0, bytes_accessed=2200000, transcendentals=0),
        name="fetch",
    )(
        ma_place.reshape(1),
        pltpu.with_memory_space_constraint(table, pltpu.HBM),
        pltpu.with_memory_space_constraint(visibility, pltpu.HBM),
    )
    (partial_spectrum,) = call(
        lambda *refs: time_kernel(nfreq, ma_count // 2, *refs),
        [((ma_count, rows, base_half), BF16)],
        [SMEM, VMEM, VMEM, VMEM],
        ma_place.reshape(1),
        near,
        own.reshape(-1, base_half),
        other.reshape(-1, base_half),
        name="time_sum",
    )
    received = lax.all_to_all(partial_spectrum, "ma", 0, 0)

    blocks = mode_dev * nfreq
    block = beam_inverse.shape[2:]
    far_beam = pltpu.with_memory_space_constraint(beam_inverse, pltpu.HBM)
    weight, *near_blocks = pl.pallas_call(
        lambda *refs: side_kernel(nfreq, *refs),
        out_shape=(pltpu.VMEM((1, base_dev), F32),) + (pltpu.VMEM(block, BF16),) * NEAR,
        in_specs=[SMEM, VMEM, ANY],
        out_specs=(VMEM,) * (1 + NEAR),
        scratch_shapes=[pltpu.SemaphoreType.DMA((NEAR,))],
        compiler_params=PARAMS,
        cost_estimate=pl.CostEstimate(
            flops=10000000, bytes_accessed=8 * 1024 * 1024, transcendentals=0
        ),
        name="side",
    )(
        (freq_place * base_dev).reshape(1),
        pltpu.with_memory_space_constraint(pair_baseline.reshape(-1, 128), pltpu.VMEM),
        far_beam,
    )
    own, send = pl.pallas_call(
        lambda *refs: beam_kernel(nfreq, *refs),
        out_shape=(pltpu.VMEM((rows, lrows), F32), pltpu.VMEM((rows, lrows), BF16)),
        in_specs=[VMEM, VMEM, ANY] + [VMEM] * NEAR,
        out_specs=(VMEM, VMEM),
        scratch_shapes=[
            pltpu.VMEM((blocks - NEAR, *block), BF16),
            pltpu.SemaphoreType.DMA((blocks - NEAR,)),
        ],
        compiler_params=PARAMS,
        name="beam",
    )(
        *(pltpu.with_memory_space_constraint(a, pltpu.VMEM) for a in (received, weight)),
        far_beam,
        *(pltpu.with_memory_space_constraint(a, pltpu.VMEM) for a in near_blocks),
    )
    outer, inner = pl.pallas_call(
        lambda *refs: table_kernel(modes, mode_dev, *refs),
        out_shape=(
            pltpu.VMEM((circles, 2, OUTER, modes), F32),
            pltpu.VMEM((circles, 2 * modes, 2 * INNER), BF16),
        ),
        in_specs=[SMEM],
        out_specs=(VMEM, VMEM),
        compiler_params=PARAMS,
        cost_estimate=pl.CostEstimate(flops=10000000, bytes_accessed=1200000, transcendentals=0),
        name="circle_tables",
    )(circle_pixels)
    arrived = [
        lax.ppermute(send, "freq", [(i, (i + k) % freq_count) for i in range(freq_count)])
        for k in range(1, freq_count)
    ]
    near_legendre = pl.pallas_call(
        legendre_fetch_kernel,
        out_shape=(pltpu.VMEM(legendre.shape, BF16),),
        in_specs=[ANY, ANY],
        out_specs=(VMEM,),
        scratch_shapes=[pltpu.SemaphoreType.DMA(())],
        compiler_params=PARAMS,
        cost_estimate=pl.CostEstimate(flops=0, bytes_accessed=4200000, transcendentals=0),
        name="legendre_fetch",
    )(own, pltpu.with_memory_space_constraint(legendre, pltpu.HBM))[0]
    latitude = pl.pallas_call(
        lambda *refs: legendre_kernel(nfreq, *refs),
        out_shape=(pltpu.VMEM((ma_count, 1, circles * rows), F32),),
        in_specs=[SMEM] + [VMEM] * 5,
        out_specs=(VMEM,),
        scratch_shapes=[pltpu.VMEM((legendre.shape[2], rows), F32)],
        compiler_params=PARAMS,
        name="legendre",
    )(
        block_rows,
        *(
            pltpu.with_memory_space_constraint(a, pltpu.VMEM)
            for a in (own, *arrived, near_legendre)
        ),
    )[0]
    regrouped = lax.all_to_all(latitude, "ma", 0, 0)
    return pl.pallas_call(
        lambda *refs: synthesis_kernel(nfreq, *refs),
        out_shape=jax.ShapeDtypeStruct((nfreq, circles, PMAX), F32),
        in_specs=[SMEM, VMEM, VMEM, VMEM],
        out_specs=VMEM,
        compiler_params=PARAMS,
        name="synthesis",
    )(
        circle_pixels,
        *(pltpu.with_memory_space_constraint(a, pltpu.VMEM) for a in (regrouped, outer, inner)),
    )


def solution(mesh):
    return jax.shard_map(
        body,
        mesh=mesh,
        in_specs=(
            P("ma", None, None, "freq"),
            P(),
            P("ma", None, None, None, "freq"),
            P("ma"),
            P("ma", None, "freq"),
            P(("freq", "ma")),
        ),
        out_specs=P(None, ("freq", "ma"), None),
        check_vma=False,
    )
```

```python
import math

import jax
import jax.numpy as jnp
import ml_dtypes
import numpy as np
from jax import lax
from jax.experimental import pallas as pl
from jax.experimental.pallas import tpu as pltpu
from jax.sharding import PartitionSpec as P

PMAX = 2048
INNER = 128
OUTER = PMAX // INNER
NEAR = 3
COS = (
    1.0, -19.739208221435547, 64.93939208984375, -85.45664978027344,
    60.24201202392578, -26.403913497924805, 7.797765254974365, -1.4502166509628296,
)
SIN = (
    6.2831854820251465, -41.34170150756836, 81.6052474975586, -76.70579528808594,
    42.057708740234375, -15.086281776428223, 3.7804296016693115, -0.6196905970573425,
)
BF16 = jnp.bfloat16
F32 = jnp.float32
SMEM = pl.BlockSpec(memory_space=pltpu.SMEM)
VMEM = pl.BlockSpec(memory_space=pltpu.VMEM)
ANY = pl.BlockSpec(memory_space=pl.ANY)
PARAMS = pltpu.CompilerParams(vmem_limit_bytes=16 * 1024 * 1024)


def split(x):
    high = x.astype(BF16)
    return high, (x - high.astype(F32)).astype(BF16)


def iota(shape, dimension):
    return lax.broadcasted_iota(jnp.int32, shape, dimension)


def polynomial(square, terms):
    total = jnp.full_like(square, terms[-1])
    for term in terms[-2::-1]:
        total = total * square + term
    return total


def cos_sin(phase, period, inverse):
    rest = phase - jnp.round(phase * inverse) * period
    turn = rest * inverse
    square = turn * turn
    return polynomial(square, COS), polynomial(square, SIN) * turn


def dot(a, b, contract):
    return lax.dot_general(a, b, ((contract[:1], contract[1:]), ((), ())), preferred_element_type=F32)


def call(kernel, outs, specs, *args, name=None):
    args = [
        pltpu.with_memory_space_constraint(a, pltpu.VMEM) if s is VMEM else a
        for a, s in zip(args, specs)
    ]
    return pl.pallas_call(
        kernel,
        out_shape=tuple(pltpu.VMEM(s, d) for s, d in outs),
        in_specs=list(specs),
        out_specs=tuple(VMEM for _ in outs),
        compiler_params=PARAMS,
        name=name,
    )(*args)


def phase_table(modes, nfreq, chip_times, ntime):
    row = np.arange(2 * modes * nfreq)[:, None]
    column = np.arange(chip_times * 2 * nfreq)[None, :]
    part_out, mode, freq_out = row // (modes * nfreq), row // nfreq % modes, row % nfreq
    time, part_in, freq_in = column // (2 * nfreq), column // nfreq % 2, column % nfreq
    phase = (mode * time + (part_out - part_in) * (ntime // 4)) % ntime
    value = np.cos(phase * (2.0 * math.pi / ntime)) / math.sqrt(ntime) * (freq_out == freq_in)
    high = value.astype(ml_dtypes.bfloat16)
    low = (value - high.astype(np.float64)).astype(ml_dtypes.bfloat16)
    return np.stack([high, low])


def fetch_kernel(place_ref, table_ref, signal_ref, near_ref, own_ref, semaphores):
    width = own_ref.shape[3]
    start = pl.multiple_of(place_ref[0] % 2 * width, width)
    copies = [
        pltpu.make_async_copy(
            signal_ref.at[:, :, :, pl.ds(start, width)], own_ref, semaphores.at[0]
        ),
        pltpu.make_async_copy(table_ref, near_ref, semaphores.at[1]),
    ]
    for copy in copies:
        copy.start()
    for copy in copies:
        copy.wait()


def time_kernel(nfreq, chips, place_ref, table_ref, own_ref, other_ref, out_ref):
    even = place_ref[0] % 2 == 0
    own, other = own_ref[...], other_ref[...]
    signal = jnp.concatenate([jnp.where(even, own, other), jnp.where(even, other, own)], 0)
    total = dot(table_ref[0], signal, (1, 0)) + dot(table_ref[1], signal, (1, 0))
    sources, rows, width = out_ref.shape
    phase = iota((chips * nfreq, width), 0) // nfreq * (place_ref[0] // 2)
    turn = ((phase + chips // 2) % chips - chips // 2).astype(F32) * (1.0 / chips)
    square = turn * turn
    cosine, sine = polynomial(square, COS)[None], (polynomial(square, SIN) * turn)[None]
    real, imag = total.reshape(2, -1, chips * nfreq, width)
    shape = (sources, rows // 2, width)
    real, imag = real * cosine + imag * sine, imag * cosine - real * sine
    out_ref[...] = jnp.concatenate([real.reshape(shape), imag.reshape(shape)], 1).astype(BF16)


def side_kernel(nfreq, first_ref, pair_ref, beam_ref, weight_ref, *refs):
    *block_refs, semaphores = refs
    copies = fetch_blocks(nfreq, beam_ref, 0, block_refs, semaphores)
    shape = (weight_ref.shape[1], pair_ref.shape[1])
    ids = iota(shape, 0) + first_ref[0]
    total = jnp.zeros(shape, F32)
    for i in range(pair_ref.shape[0]):
        total += jnp.where(pair_ref[i : i + 1, :] == ids, 1.0, 0.0)
    weight_ref[...] = jnp.sqrt(jnp.sum(total.T, 0, keepdims=True))
    for copy in copies:
        copy.wait()


def fetch_blocks(nfreq, beam_ref, first, block_refs, semaphores):
    copies = [
        pltpu.make_async_copy(
            beam_ref.at[(first + i) // nfreq, (first + i) % nfreq], block_ref, semaphores.at[i]
        )
        for i, block_ref in enumerate(block_refs)
    ]
    for copy in copies:
        copy.start()
    return copies


def beam_kernel(nfreq, part_ref, weight_ref, beam_ref, *refs):
    *near_refs, total_ref, send_ref, far_ref, semaphores = refs
    near = len(near_refs)
    far_refs = [far_ref.at[i] for i in range(far_ref.shape[0])]
    copies = fetch_blocks(nfreq, beam_ref, near, far_refs, semaphores)
    sources, rows, width = part_ref.shape
    half = rows // 2
    sums = part_ref[...].astype(F32).reshape(sources // 2, 2, rows, width).sum(0)
    weighted = jnp.concatenate([sums[0], sums[1]], 1) * weight_ref[...]
    turned = jnp.concatenate([-weighted[half:], weighted[:half]], 0)
    row = iota((2 * rows, weighted.shape[1]), 0) % half
    lefts = [jnp.concatenate(split(value), 0) for value in (weighted, turned)]
    total = jnp.zeros((2 * rows, total_ref.shape[1]), F32)
    for i, block_ref in enumerate([*near_refs, *far_refs]):
        if i >= near:
            copies[i - near].wait()
        for c in range(2):
            left = jnp.where(row == i, lefts[c], jnp.zeros_like(lefts[c]))
            total += dot(left, block_ref[c], (1, 1))
    total = total[:rows] + total[rows:]
    total_ref[...] = total
    send_ref[...] = total.astype(BF16)


def legendre_kernel(
    nfreq, rows_ref, own_ref, first_ref, second_ref, third_ref, table_ref, out_ref, scratch_ref
):
    total = own_ref[...] + first_ref[...].astype(F32)
    total = total + second_ref[...].astype(F32) + third_ref[...].astype(F32)
    rows = total.shape[0]
    left = jnp.concatenate(split(total), 0)
    row = iota(left.shape, 0) // nfreq
    column = iota(left.shape, 1)
    modes = table_ref.shape[0]
    latitude = jnp.zeros((2 * rows, table_ref.shape[2]), F32)
    for m in range(modes):
        live = (row % modes == m) & (column < rows_ref[m])
        latitude += dot(jnp.where(live, left, jnp.zeros_like(left)), table_ref[m], (1, 0))
    scratch_ref[...] = (latitude[:rows] + latitude[rows:]).T
    dests, _, width = out_ref.shape
    circles = scratch_ref.shape[0] // dests
    pieces = [scratch_ref[pl.ds(j, dests, circles), :] for j in range(circles)]
    out_ref[...] = jnp.concatenate(pieces, 1).reshape(out_ref.shape)


def mode_of(position, modes, mode_dev):
    blocks = modes // mode_dev
    return position % blocks * mode_dev + position // blocks


def table_kernel(modes, mode_dev, count_ref, outer_ref, inner_ref):
    for circle in range(count_ref.shape[0]):
        period = jnp.full((1, 1), 2 * count_ref[circle], jnp.int32).astype(F32)
        inverse = 1.0 / period
        mode = mode_of(iota((OUTER, modes), 1), modes, mode_dev)
        step = iota((OUTER, modes), 0) * (2 * INNER)
        outer_ref[circle, 0], outer_ref[circle, 1] = cos_sin(
            (mode * step).astype(F32), period, inverse
        )
        blocks = modes // mode_dev
        mode = iota((blocks, INNER), 0) * mode_dev
        step = iota((blocks, INNER), 1) * 2 + 1
        cosine, sine = cos_sin((mode * step).astype(F32), period, inverse)
        first = jnp.where(mode == 0, 1.0, 2.0)
        small = (8, INNER)
        small_step = (iota(small, 0) * (iota(small, 1) * 2 + 1)).astype(F32)
        turn_cosine, turn_sine = cos_sin(small_step, period, inverse)
        for j in range(mode_dev):
            c, s = turn_cosine[j : j + 1], turn_sine[j : j + 1]
            factor = first if j == 0 else 2.0
            for part, value in enumerate(
                ((cosine * c - sine * s) * factor, (sine * c + cosine * s) * -factor)
            ):
                high, low = split(value)
                at = part * modes + j * blocks
                inner_ref[circle, at : at + blocks, :INNER] = high
                inner_ref[circle, at : at + blocks, INNER:] = low


def middle_kernel(
    modes, mode_dev, count_ref, after_ref, legendre_ref,
    near_ref, outer_ref, inner_ref, semaphore,
):
    del after_ref
    copy = pltpu.make_async_copy(legendre_ref, near_ref, semaphore)
    copy.start()
    table_kernel(modes, mode_dev, count_ref, outer_ref, inner_ref)
    copy.wait()


def synthesis_kernel(nfreq, count_ref, value_ref, outer_ref, inner_ref, map_ref):
    circles = outer_ref.shape[0]
    sources, _, width = value_ref.shape
    values = value_ref[...].reshape(sources, width).T
    each = width // circles
    results = []
    for circle in range(circles):
        cosine = outer_ref[circle, 0]
        sine = outer_ref[circle, 1]
        rows = []
        for f in range(nfreq):
            start = circle * each + f
            real, imag = (
                jnp.concatenate([values[i : i + 1] for i in range(at, at + each // 2, nfreq)], 1)
                for at in (start, start + each // 2)
            )
            rows.append(
                jnp.concatenate([real * cosine - imag * sine, real * sine + imag * cosine], 1)
            )
        high, low = split(jnp.concatenate(rows, 0))
        result = dot(jnp.concatenate([high, low], 0), inner_ref[circle], (1, 0))
        half = nfreq * OUTER
        results.append(
            result[:half, :INNER] + (result[:half, INNER:] + result[half:, :INNER])
        )
    pixel = iota((OUTER, INNER), 0) * INNER + iota((OUTER, INNER), 1)
    for circle in range(circles):
        keep = pixel < count_ref[circle]
        for f in range(nfreq):
            part = jnp.where(keep, results[circle][f * OUTER : (f + 1) * OUTER], 0.0)
            for q in range(OUTER):
                map_ref[f, circle : circle + 1, q * INNER : (q + 1) * INNER] = part[q : q + 1]


def body(visibility, pair_baseline, beam_inverse, block_rows, legendre, circle_pixels):
    ma_count = lax.axis_size("ma")
    freq_count = lax.axis_size("freq")
    ma_place = lax.axis_index("ma")
    freq_place = lax.axis_index("freq")
    time_dev, _, nfreq, base_dev = visibility.shape
    ntime = time_dev * ma_count
    mode_dev, _, _, lrows, _ = beam_inverse.shape
    modes = mode_dev * ma_count
    circles = circle_pixels.shape[0]
    base_half = base_dev // 2
    rows = mode_dev * 2 * nfreq

    other = lax.ppermute(visibility, "ma", [(i, i ^ 1) for i in range(ma_count)])
    other = lax.dynamic_slice_in_dim(other, ma_place % 2 * base_half, base_half, 3)
    table = jnp.asarray(phase_table(modes, nfreq, 2 * time_dev, ntime))
    near, own = pl.pallas_call(
        fetch_kernel,
        out_shape=(pltpu.VMEM(table.shape, BF16), pltpu.VMEM(other.shape, BF16)),
        in_specs=[SMEM, ANY, ANY],
        out_specs=(VMEM, VMEM),
        scratch_shapes=[pltpu.SemaphoreType.DMA((2,))],
        compiler_params=PARAMS,
        cost_estimate=pl.CostEstimate(flops=0, bytes_accessed=2200000, transcendentals=0),
        name="fetch",
    )(
        ma_place.reshape(1),
        pltpu.with_memory_space_constraint(table, pltpu.HBM),
        pltpu.with_memory_space_constraint(visibility, pltpu.HBM),
    )
    (partial_spectrum,) = call(
        lambda *refs: time_kernel(nfreq, ma_count // 2, *refs),
        [((ma_count, rows, base_half), BF16)],
        [SMEM, VMEM, VMEM, VMEM],
        ma_place.reshape(1),
        near,
        own.reshape(-1, base_half),
        other.reshape(-1, base_half),
        name="time_sum",
    )
    received = lax.all_to_all(partial_spectrum, "ma", 0, 0)

    blocks = mode_dev * nfreq
    block = beam_inverse.shape[2:]
    far_beam = pltpu.with_memory_space_constraint(beam_inverse, pltpu.HBM)
    weight, *near_blocks = pl.pallas_call(
        lambda *refs: side_kernel(nfreq, *refs),
        out_shape=(pltpu.VMEM((1, base_dev), F32),) + (pltpu.VMEM(block, BF16),) * NEAR,
        in_specs=[SMEM, VMEM, ANY],
        out_specs=(VMEM,) * (1 + NEAR),
        scratch_shapes=[pltpu.SemaphoreType.DMA((NEAR,))],
        compiler_params=PARAMS,
        cost_estimate=pl.CostEstimate(
            flops=10000000, bytes_accessed=8 * 1024 * 1024, transcendentals=0
        ),
        name="side",
    )(
        (freq_place * base_dev).reshape(1),
        pltpu.with_memory_space_constraint(pair_baseline.reshape(-1, 128), pltpu.VMEM),
        far_beam,
    )
    own, send = pl.pallas_call(
        lambda *refs: beam_kernel(nfreq, *refs),
        out_shape=(pltpu.VMEM((rows, lrows), F32), pltpu.VMEM((rows, lrows), BF16)),
        in_specs=[VMEM, VMEM, ANY] + [VMEM] * NEAR,
        out_specs=(VMEM, VMEM),
        scratch_shapes=[
            pltpu.VMEM((blocks - NEAR, *block), BF16),
            pltpu.SemaphoreType.DMA((blocks - NEAR,)),
        ],
        compiler_params=PARAMS,
        name="beam",
    )(
        *(pltpu.with_memory_space_constraint(a, pltpu.VMEM) for a in (received, weight)),
        far_beam,
        *(pltpu.with_memory_space_constraint(a, pltpu.VMEM) for a in near_blocks),
    )
    arrived = [
        lax.ppermute(send, "freq", [(i, (i + k) % freq_count) for i in range(freq_count)])
        for k in range(1, freq_count)
    ]
    near_legendre, outer, inner = pl.pallas_call(
        lambda *refs: middle_kernel(modes, mode_dev, *refs),
        out_shape=(
            pltpu.VMEM(legendre.shape, BF16),
            pltpu.VMEM((circles, 2, OUTER, modes), F32),
            pltpu.VMEM((circles, 2 * modes, 2 * INNER), BF16),
        ),
        in_specs=[SMEM, ANY, ANY],
        out_specs=(VMEM,) * 3,
        scratch_shapes=[pltpu.SemaphoreType.DMA(())],
        compiler_params=PARAMS,
        cost_estimate=pl.CostEstimate(
            flops=10000000, bytes_accessed=4200000, transcendentals=0
        ),
        name="middle",
    )(circle_pixels, own, pltpu.with_memory_space_constraint(legendre, pltpu.HBM))
    latitude = pl.pallas_call(
        lambda *refs: legendre_kernel(nfreq, *refs),
        out_shape=(pltpu.VMEM((ma_count, 1, circles * rows), F32),),
        in_specs=[SMEM] + [VMEM] * 5,
        out_specs=(VMEM,),
        scratch_shapes=[pltpu.VMEM((legendre.shape[2], rows), F32)],
        compiler_params=PARAMS,
        name="legendre",
    )(
        block_rows,
        *(
            pltpu.with_memory_space_constraint(a, pltpu.VMEM)
            for a in (own, *arrived, near_legendre)
        ),
    )[0]
    regrouped = lax.all_to_all(latitude, "ma", 0, 0)
    return pl.pallas_call(
        lambda *refs: synthesis_kernel(nfreq, *refs),
        out_shape=jax.ShapeDtypeStruct((nfreq, circles, PMAX), F32),
        in_specs=[SMEM, VMEM, VMEM, VMEM],
        out_specs=VMEM,
        compiler_params=PARAMS,
        name="synthesis",
    )(
        circle_pixels,
        *(pltpu.with_memory_space_constraint(a, pltpu.VMEM) for a in (regrouped, outer, inner)),
    )


def solution(mesh):
    return jax.shard_map(
        body,
        mesh=mesh,
        in_specs=(
            P("ma", None, None, "freq"),
            P(),
            P("ma", None, None, None, "freq"),
            P("ma"),
            P("ma", None, "freq"),
            P(("freq", "ma")),
        ),
        out_specs=P(None, ("freq", "ma"), None),
        check_vma=False,
    )
```

```python
import math

import jax
import jax.numpy as jnp
import ml_dtypes
import numpy as np
from jax import lax
from jax.experimental import pallas as pl
from jax.experimental.pallas import tpu as pltpu
from jax.sharding import PartitionSpec as P

PMAX = 2048
INNER = 128
OUTER = PMAX // INNER
NEAR = 3
COS = (
    1.0, -19.739208221435547, 64.93939208984375, -85.45664978027344,
    60.24201202392578, -26.403913497924805, 7.797765254974365, -1.4502166509628296,
)
SIN = (
    6.2831854820251465, -41.34170150756836, 81.6052474975586, -76.70579528808594,
    42.057708740234375, -15.086281776428223, 3.7804296016693115, -0.6196905970573425,
)
BF16 = jnp.bfloat16
F32 = jnp.float32
SMEM = pl.BlockSpec(memory_space=pltpu.SMEM)
VMEM = pl.BlockSpec(memory_space=pltpu.VMEM)
ANY = pl.BlockSpec(memory_space=pl.ANY)
PARAMS = pltpu.CompilerParams(vmem_limit_bytes=16 * 1024 * 1024)


def split(x):
    high = x.astype(BF16)
    return high, (x - high.astype(F32)).astype(BF16)


def iota(shape, dimension):
    return lax.broadcasted_iota(jnp.int32, shape, dimension)


def polynomial(square, terms):
    total = jnp.full_like(square, terms[-1])
    for term in terms[-2::-1]:
        total = total * square + term
    return total


def cos_sin(phase, period, inverse):
    rest = phase - jnp.round(phase * inverse) * period
    turn = rest * inverse
    square = turn * turn
    return polynomial(square, COS), polynomial(square, SIN) * turn


def dot(a, b, contract):
    return lax.dot_general(a, b, ((contract[:1], contract[1:]), ((), ())), preferred_element_type=F32)


def call(kernel, outs, specs, *args, name=None):
    args = [
        pltpu.with_memory_space_constraint(a, pltpu.VMEM) if s is VMEM else a
        for a, s in zip(args, specs)
    ]
    return pl.pallas_call(
        kernel,
        out_shape=tuple(pltpu.VMEM(s, d) for s, d in outs),
        in_specs=list(specs),
        out_specs=tuple(VMEM for _ in outs),
        compiler_params=PARAMS,
        name=name,
    )(*args)


def phase_table(modes, mode_dev, nfreq, chip_times, ntime):
    half = modes // 2
    row = np.arange(2 * half * nfreq)[:, None]
    column = np.arange(chip_times * 2 * nfreq)[None, :]
    part_out, place, freq_out = row // (half * nfreq), row // nfreq % half, row % nfreq
    time, part_in, freq_in = column // (2 * nfreq), column // nfreq % 2, column % nfreq
    tables = []
    for core in range(2):
        mode = place // mode_dev * (2 * mode_dev) + core * mode_dev + place % mode_dev
        phase = (mode * time + (part_out - part_in) * (ntime // 4)) % ntime
        value = np.cos(phase * (2.0 * math.pi / ntime)) / math.sqrt(ntime)
        value = value * (freq_out == freq_in)
        high = value.astype(ml_dtypes.bfloat16)
        low = (value - high.astype(np.float64)).astype(ml_dtypes.bfloat16)
        tables.append(np.stack([high, low]))
    return np.stack(tables)


def fetch_kernel(table_ref, signal_ref, near_ref, left_ref, right_ref, semaphores):
    width = left_ref.shape[3]
    copies = [
        pltpu.make_async_copy(
            signal_ref.at[:, :, :, :width], left_ref, semaphores.at[0]
        ),
        pltpu.make_async_copy(
            signal_ref.at[:, :, :, width:], right_ref, semaphores.at[1]
        ),
        pltpu.make_async_copy(
            table_ref.at[lax.rem(lax.axis_index("ma"), 2)], near_ref, semaphores.at[2]
        ),
    ]
    for copy in copies:
        copy.start()
    for copy in copies:
        copy.wait()


def time_kernel(nfreq, chips, mode_dev, table_ref, *refs):
    *signal_refs, out_ref = refs
    place = lax.axis_index("ma")
    core = lax.rem(place, 2)
    own_left, own_right, other_left, other_right = (ref[...] for ref in signal_refs)
    own = jnp.concatenate([own_left, own_right], 1)
    other = jnp.concatenate([other_left, other_right], 1)
    even = core == 0
    signal = jnp.concatenate([jnp.where(even, own, other), jnp.where(even, other, own)], 0)
    total = dot(table_ref[0], signal, (1, 0)) + dot(table_ref[1], signal, (1, 0))
    dests, rows, width = out_ref.shape
    period = chips // 2 * nfreq
    index = iota((period, width), 0) // nfreq
    mode = index // mode_dev * (2 * mode_dev) + core * mode_dev + index % mode_dev
    phase = mode * lax.div(place, 2)
    turn = ((phase + chips // 2) % chips - chips // 2).astype(F32) * (1.0 / chips)
    square = turn * turn
    cosine, sine = polynomial(square, COS)[None], (polynomial(square, SIN) * turn)[None]
    real, imag = total.reshape(2, -1, period, width)
    shape = (dests, rows // 2, width)
    real, imag = real * cosine + imag * sine, imag * cosine - real * sine
    out_ref[...] = jnp.concatenate([real.reshape(shape), imag.reshape(shape)], 1).astype(BF16)


def side_kernel(nfreq, pair_ref, beam_ref, weight_ref, *refs):
    *block_refs, semaphores = refs
    copies = fetch_blocks(nfreq, beam_ref, 0, block_refs, semaphores)
    shape = (weight_ref.shape[1], pair_ref.shape[1])
    ids = iota(shape, 0) + lax.axis_index("freq") * shape[0]
    total = jnp.zeros(shape, F32)
    for i in range(pair_ref.shape[0]):
        total += jnp.where(pair_ref[i : i + 1, :] == ids, 1.0, 0.0)
    weight_ref[...] = jnp.sqrt(jnp.sum(total.T, 0, keepdims=True))
    for copy in copies:
        copy.wait()


def fetch_blocks(nfreq, beam_ref, first, block_refs, semaphores):
    copies = [
        pltpu.make_async_copy(
            beam_ref.at[(first + i) // nfreq, (first + i) % nfreq], block_ref, semaphores.at[i]
        )
        for i, block_ref in enumerate(block_refs)
    ]
    for copy in copies:
        copy.start()
    return copies


def beam_kernel(nfreq, part_ref, weight_ref, beam_ref, *refs):
    *near_refs, total_ref, send_ref, far_ref, semaphores = refs
    near = len(near_refs)
    far_refs = [far_ref.at[i] for i in range(far_ref.shape[0])]
    copies = fetch_blocks(nfreq, beam_ref, near, far_refs, semaphores)
    rows = part_ref.shape[1]
    half = rows // 2
    weighted = part_ref[...].astype(F32).sum(0) * weight_ref[...]
    turned = jnp.concatenate([-weighted[half:], weighted[:half]], 0)
    row = iota((2 * rows, weighted.shape[1]), 0) % half
    lefts = [jnp.concatenate(split(value), 0) for value in (weighted, turned)]
    total = jnp.zeros((2 * rows, total_ref.shape[1]), F32)
    for i, block_ref in enumerate([*near_refs, *far_refs]):
        if i >= near:
            copies[i - near].wait()
        for c in range(2):
            left = jnp.where(row == i, lefts[c], jnp.zeros_like(lefts[c]))
            total += dot(left, block_ref[c], (1, 1))
    total = total[:rows] + total[rows:]
    total_ref[...] = total
    send_ref[...] = total.astype(BF16)


def legendre_kernel(
    nfreq, rows_ref, own_ref, first_ref, second_ref, third_ref, table_ref, out_ref, scratch_ref
):
    total = own_ref[...] + first_ref[...].astype(F32)
    total = total + second_ref[...].astype(F32) + third_ref[...].astype(F32)
    rows = total.shape[0]
    left = jnp.concatenate(split(total), 0)
    row = iota(left.shape, 0) // nfreq
    column = iota(left.shape, 1)
    modes = table_ref.shape[0]
    latitude = jnp.zeros((2 * rows, table_ref.shape[2]), F32)
    for m in range(modes):
        live = (row % modes == m) & (column < rows_ref[m])
        latitude += dot(jnp.where(live, left, jnp.zeros_like(left)), table_ref[m], (1, 0))
    latitude = (latitude[:rows] + latitude[rows:]).T
    scratch_ref[: latitude.shape[0]] = latitude
    dests, _, width = out_ref.shape
    circles = latitude.shape[0] // dests
    pieces = [scratch_ref[pl.ds(j, dests, circles), :] for j in range(circles)]
    out_ref[...] = jnp.concatenate(pieces, 1).reshape(out_ref.shape)


def mode_of(position, modes, mode_dev):
    blocks = modes // mode_dev
    return position % blocks * mode_dev + position // blocks


def table_kernel(modes, mode_dev, count_ref, outer_ref, inner_ref):
    for circle in range(count_ref.shape[0]):
        period = jnp.full((1, 1), 2 * count_ref[circle], jnp.int32).astype(F32)
        inverse = 1.0 / period
        mode = mode_of(iota((OUTER, modes), 1), modes, mode_dev)
        step = iota((OUTER, modes), 0) * (2 * INNER)
        outer_ref[circle, 0], outer_ref[circle, 1] = cos_sin(
            (mode * step).astype(F32), period, inverse
        )
        blocks = modes // mode_dev
        mode = iota((blocks, INNER), 0) * mode_dev
        step = iota((blocks, INNER), 1) * 2 + 1
        cosine, sine = cos_sin((mode * step).astype(F32), period, inverse)
        first = jnp.where(mode == 0, 1.0, 2.0)
        small = (8, INNER)
        small_step = (iota(small, 0) * (iota(small, 1) * 2 + 1)).astype(F32)
        turn_cosine, turn_sine = cos_sin(small_step, period, inverse)
        for j in range(mode_dev):
            c, s = turn_cosine[j : j + 1], turn_sine[j : j + 1]
            factor = first if j == 0 else 2.0
            for part, value in enumerate(
                ((cosine * c - sine * s) * factor, (sine * c + cosine * s) * -factor)
            ):
                high, low = split(value)
                at = part * modes + j * blocks
                inner_ref[circle, at : at + blocks, :INNER] = high
                inner_ref[circle, at : at + blocks, INNER:] = low


def middle_kernel(
    modes, mode_dev, count_ref, after_ref, legendre_ref,
    near_ref, outer_ref, inner_ref, semaphore,
):
    del after_ref
    copy = pltpu.make_async_copy(legendre_ref, near_ref, semaphore)
    copy.start()
    table_kernel(modes, mode_dev, count_ref, outer_ref, inner_ref)
    copy.wait()


def synthesis_kernel(nfreq, count_ref, value_ref, outer_ref, inner_ref, map_ref):
    circles = outer_ref.shape[0]
    sources, _, width = value_ref.shape
    values = value_ref[...].reshape(sources, width).T
    each = width // circles
    results = []
    for circle in range(circles):
        cosine = outer_ref[circle, 0]
        sine = outer_ref[circle, 1]
        rows = []
        for f in range(nfreq):
            start = circle * each + f
            real, imag = (
                jnp.concatenate([values[i : i + 1] for i in range(at, at + each // 2, nfreq)], 1)
                for at in (start, start + each // 2)
            )
            rows.append(
                jnp.concatenate([real * cosine - imag * sine, real * sine + imag * cosine], 1)
            )
        high, low = split(jnp.concatenate(rows, 0))
        result = dot(jnp.concatenate([high, low], 0), inner_ref[circle], (1, 0))
        half = nfreq * OUTER
        results.append(
            result[:half, :INNER] + (result[:half, INNER:] + result[half:, :INNER])
        )
    pixel = iota((OUTER, INNER), 0) * INNER + iota((OUTER, INNER), 1)
    for circle in range(circles):
        keep = pixel < count_ref[circle]
        for f in range(nfreq):
            part = jnp.where(keep, results[circle][f * OUTER : (f + 1) * OUTER], 0.0)
            for q in range(OUTER):
                map_ref[f, circle : circle + 1, q * INNER : (q + 1) * INNER] = part[q : q + 1]


def body(visibility, pair_baseline, beam_inverse, block_rows, legendre, circle_pixels):
    ma_count = lax.axis_size("ma")
    freq_count = lax.axis_size("freq")
    time_dev, _, nfreq, base_dev = visibility.shape
    ntime = time_dev * ma_count
    mode_dev, _, _, lrows, _ = beam_inverse.shape
    modes = mode_dev * ma_count
    circles = circle_pixels.shape[0]
    base_half = base_dev // 2
    rows = mode_dev * 2 * nfreq

    other = lax.ppermute(visibility, "ma", [(i, i ^ 1) for i in range(ma_count)])
    table = jnp.asarray(phase_table(modes, mode_dev, nfreq, 2 * time_dev, ntime))
    piece = (time_dev, 2, nfreq, base_half)
    near, left, right = pl.pallas_call(
        fetch_kernel,
        out_shape=(
            pltpu.VMEM(table.shape[1:], BF16),
            pltpu.VMEM(piece, BF16),
            pltpu.VMEM(piece, BF16),
        ),
        in_specs=[ANY, ANY],
        out_specs=(VMEM,) * 3,
        scratch_shapes=[pltpu.SemaphoreType.DMA((3,))],
        compiler_params=PARAMS,
        cost_estimate=pl.CostEstimate(flops=0, bytes_accessed=1200000, transcendentals=0),
        name="fetch",
    )(
        pltpu.with_memory_space_constraint(table, pltpu.HBM),
        pltpu.with_memory_space_constraint(visibility, pltpu.HBM),
    )
    (partial_spectrum,) = call(
        lambda *refs: time_kernel(nfreq, ma_count // 2, mode_dev, *refs),
        [((ma_count // 2, rows, base_dev), BF16)],
        [VMEM] * 5,
        near,
        *(
            a.reshape(-1, base_half)
            for a in (left, right, other[..., :base_half], other[..., base_half:])
        ),
        name="time_sum",
    )
    groups = [list(range(core, ma_count, 2)) for core in range(2)]
    received = lax.all_to_all(partial_spectrum, "ma", 0, 0, axis_index_groups=groups)

    blocks = mode_dev * nfreq
    block = beam_inverse.shape[2:]
    far_beam = pltpu.with_memory_space_constraint(beam_inverse, pltpu.HBM)
    weight, *near_blocks = pl.pallas_call(
        lambda *refs: side_kernel(nfreq, *refs),
        out_shape=(pltpu.VMEM((1, base_dev), F32),) + (pltpu.VMEM(block, BF16),) * NEAR,
        in_specs=[VMEM, ANY],
        out_specs=(VMEM,) * (1 + NEAR),
        scratch_shapes=[pltpu.SemaphoreType.DMA((NEAR,))],
        compiler_params=PARAMS,
        cost_estimate=pl.CostEstimate(
            flops=10000000, bytes_accessed=8 * 1024 * 1024, transcendentals=0
        ),
        name="side",
    )(
        pltpu.with_memory_space_constraint(pair_baseline.reshape(-1, 128), pltpu.VMEM),
        far_beam,
    )
    own, send = pl.pallas_call(
        lambda *refs: beam_kernel(nfreq, *refs),
        out_shape=(pltpu.VMEM((rows, lrows), F32), pltpu.VMEM((rows, lrows), BF16)),
        in_specs=[VMEM, VMEM, ANY] + [VMEM] * NEAR,
        out_specs=(VMEM, VMEM),
        scratch_shapes=[
            pltpu.VMEM((blocks - NEAR, *block), BF16),
            pltpu.SemaphoreType.DMA((blocks - NEAR,)),
        ],
        compiler_params=PARAMS,
        name="beam",
    )(
        *(pltpu.with_memory_space_constraint(a, pltpu.VMEM) for a in (received, weight)),
        far_beam,
        *(pltpu.with_memory_space_constraint(a, pltpu.VMEM) for a in near_blocks),
    )
    arrived = [
        lax.ppermute(send, "freq", [(i, (i + k) % freq_count) for i in range(freq_count)])
        for k in range(1, freq_count)
    ]
    near_legendre, outer, inner = pl.pallas_call(
        lambda *refs: middle_kernel(modes, mode_dev, *refs),
        out_shape=(
            pltpu.VMEM(legendre.shape, BF16),
            pltpu.VMEM((circles, 2, OUTER, modes), F32),
            pltpu.VMEM((circles, 2 * modes, 2 * INNER), BF16),
        ),
        in_specs=[SMEM, ANY, ANY],
        out_specs=(VMEM,) * 3,
        scratch_shapes=[pltpu.SemaphoreType.DMA(())],
        compiler_params=PARAMS,
        cost_estimate=pl.CostEstimate(
            flops=10000000, bytes_accessed=4200000, transcendentals=0
        ),
        name="middle",
    )(circle_pixels, own, pltpu.with_memory_space_constraint(legendre, pltpu.HBM))
    latitude = pl.pallas_call(
        lambda *refs: legendre_kernel(nfreq, *refs),
        out_shape=(pltpu.VMEM((ma_count, 1, circles * rows), F32),),
        in_specs=[SMEM] + [VMEM] * 5,
        out_specs=(VMEM,),
        scratch_shapes=[pltpu.VMEM((legendre.shape[2] + 8, rows), F32)],
        compiler_params=PARAMS,
        name="legendre",
    )(
        block_rows,
        *(
            pltpu.with_memory_space_constraint(a, pltpu.VMEM)
            for a in (own, *arrived, near_legendre)
        ),
    )[0]
    regrouped = lax.all_to_all(latitude, "ma", 0, 0)
    return pl.pallas_call(
        lambda *refs: synthesis_kernel(nfreq, *refs),
        out_shape=jax.ShapeDtypeStruct((nfreq, circles, PMAX), F32),
        in_specs=[SMEM, VMEM, VMEM, VMEM],
        out_specs=VMEM,
        compiler_params=PARAMS,
        name="synthesis",
    )(
        circle_pixels,
        *(pltpu.with_memory_space_constraint(a, pltpu.VMEM) for a in (regrouped, outer, inner)),
    )


def solution(mesh):
    return jax.shard_map(
        body,
        mesh=mesh,
        in_specs=(
            P("ma", None, None, "freq"),
            P(),
            P("ma", None, None, None, "freq"),
            P("ma"),
            P("ma", None, "freq"),
            P(("freq", "ma")),
        ),
        out_specs=P(None, ("freq", "ma"), None),
        check_vma=False,
    )
```

```python
import math

import jax
import jax.numpy as jnp
import ml_dtypes
import numpy as np
from jax import lax
from jax.experimental import pallas as pl
from jax.experimental.pallas import tpu as pltpu
from jax.sharding import PartitionSpec as P

PMAX = 2048
INNER = 128
OUTER = PMAX // INNER
NEAR = 3
COS = (
    1.0, -19.739208221435547, 64.93939208984375, -85.45664978027344,
    60.24201202392578, -26.403913497924805, 7.797765254974365, -1.4502166509628296,
)
SIN = (
    6.2831854820251465, -41.34170150756836, 81.6052474975586, -76.70579528808594,
    42.057708740234375, -15.086281776428223, 3.7804296016693115, -0.6196905970573425,
)
BF16 = jnp.bfloat16
F32 = jnp.float32
SMEM = pl.BlockSpec(memory_space=pltpu.SMEM)
VMEM = pl.BlockSpec(memory_space=pltpu.VMEM)
ANY = pl.BlockSpec(memory_space=pl.ANY)
PARAMS = pltpu.CompilerParams(vmem_limit_bytes=16 * 1024 * 1024)


def split(x):
    high = x.astype(BF16)
    return high, (x - high.astype(F32)).astype(BF16)


def iota(shape, dimension):
    return lax.broadcasted_iota(jnp.int32, shape, dimension)


def polynomial(square, terms):
    total = jnp.full_like(square, terms[-1])
    for term in terms[-2::-1]:
        total = total * square + term
    return total


def cos_sin(phase, period, inverse):
    rest = phase - jnp.round(phase * inverse) * period
    turn = rest * inverse
    square = turn * turn
    return polynomial(square, COS), polynomial(square, SIN) * turn


def dot(a, b, contract):
    return lax.dot_general(a, b, ((contract[:1], contract[1:]), ((), ())), preferred_element_type=F32)


def phase_table(modes, mode_dev, nfreq, chip_times, ntime):
    half = modes // 2
    row = np.arange(2 * half * nfreq)[:, None]
    column = np.arange(chip_times * 2 * nfreq)[None, :]
    part_out, place, freq_out = row // (half * nfreq), row // nfreq % half, row % nfreq
    time, part_in, freq_in = column // (2 * nfreq), column // nfreq % 2, column % nfreq
    tables = []
    for core in range(2):
        mode = place // mode_dev * (2 * mode_dev) + core * mode_dev + place % mode_dev
        phase = (mode * time + (part_out - part_in) * (ntime // 4)) % ntime
        value = np.cos(phase * (2.0 * math.pi / ntime)) / math.sqrt(ntime)
        value = value * (freq_out == freq_in)
        high = value.astype(ml_dtypes.bfloat16)
        low = (value - high.astype(np.float64)).astype(ml_dtypes.bfloat16)
        tables.append(np.stack([high, low]))
    return np.stack(tables)


def fetch_kernel(table_ref, signal_ref, near_ref, left_ref, right_ref, semaphores):
    width = left_ref.shape[3]
    copies = [
        pltpu.make_async_copy(
            signal_ref.at[:, :, :, :width], left_ref, semaphores.at[0]
        ),
        pltpu.make_async_copy(
            signal_ref.at[:, :, :, width:], right_ref, semaphores.at[1]
        ),
        pltpu.make_async_copy(
            table_ref.at[lax.rem(lax.axis_index("ma"), 2)], near_ref, semaphores.at[2]
        ),
    ]
    for copy in copies:
        copy.start()
    for copy in copies:
        copy.wait()


def time_kernel(nfreq, chips, mode_dev, table_ref, *refs):
    *signal_refs, out_ref, part_ref, semaphores = refs
    place = lax.axis_index("ma")
    core = lax.rem(place, 2)
    own_left, own_right, other_left, other_right = (ref[...] for ref in signal_refs)
    own = jnp.concatenate([own_left, own_right], 1)
    other = jnp.concatenate([other_left, other_right], 1)
    even = core == 0
    signal = jnp.concatenate([jnp.where(even, own, other), jnp.where(even, other, own)], 0)
    total = dot(table_ref[0], signal, (1, 0)) + dot(table_ref[1], signal, (1, 0))
    dests, rows, width = out_ref.shape
    period = chips // 2 * nfreq
    index = iota((period, width), 0) // nfreq
    mode = index // mode_dev * (2 * mode_dev) + core * mode_dev + index % mode_dev
    phase = mode * lax.div(place, 2)
    turn = ((phase + chips // 2) % chips - chips // 2).astype(F32) * (1.0 / chips)
    square = turn * turn
    cosine, sine = polynomial(square, COS)[None], (polynomial(square, SIN) * turn)[None]
    real, imag = total.reshape(2, -1, period, width)
    parts = semaphores.shape[0]
    blocks, size = real.shape[0] // parts, dests // parts
    shape = (size, rows // 2, width)
    copies = []
    for i in range(parts):
        a, b = real[i * blocks : (i + 1) * blocks], imag[i * blocks : (i + 1) * blocks]
        a, b = a * cosine + b * sine, b * cosine - a * sine
        at = pl.ds(i * size, size)
        part_ref[at] = jnp.concatenate([a.reshape(shape), b.reshape(shape)], 1).astype(BF16)
        copies.append(pltpu.make_async_copy(part_ref.at[at], out_ref.at[at], semaphores.at[i]))
        copies[i].start()
    for copy in copies:
        copy.wait()


def side_kernel(nfreq, pair_ref, beam_ref, weight_ref, *refs):
    *block_refs, semaphores = refs
    copies = fetch_blocks(nfreq, beam_ref, 0, block_refs, semaphores)
    shape = (weight_ref.shape[1], pair_ref.shape[1])
    ids = iota(shape, 0) + lax.axis_index("freq") * shape[0]
    total = jnp.zeros(shape, F32)
    for i in range(pair_ref.shape[0]):
        total += jnp.where(pair_ref[i : i + 1, :] == ids, 1.0, 0.0)
    weight_ref[...] = jnp.sqrt(jnp.sum(total.T, 0, keepdims=True))
    for copy in copies:
        copy.wait()


def fetch_blocks(nfreq, beam_ref, first, block_refs, semaphores):
    copies = [
        pltpu.make_async_copy(
            beam_ref.at[(first + i) // nfreq, (first + i) % nfreq], block_ref, semaphores.at[i]
        )
        for i, block_ref in enumerate(block_refs)
    ]
    for copy in copies:
        copy.start()
    return copies


def beam_kernel(nfreq, part_ref, weight_ref, beam_ref, *refs):
    *near_refs, total_ref, send_ref, far_ref, semaphores = refs
    near = len(near_refs)
    far_refs = [far_ref.at[i] for i in range(far_ref.shape[0])]
    copies = fetch_blocks(nfreq, beam_ref, near, far_refs, semaphores)
    rows = part_ref.shape[1]
    half = rows // 2
    weighted = part_ref[...].astype(F32).sum(0) * weight_ref[...]
    turned = jnp.concatenate([-weighted[half:], weighted[:half]], 0)
    row = iota((2 * rows, weighted.shape[1]), 0) % half
    lefts = [jnp.concatenate(split(value), 0) for value in (weighted, turned)]
    total = jnp.zeros((2 * rows, total_ref.shape[1]), F32)
    for i, block_ref in enumerate([*near_refs, *far_refs]):
        if i >= near:
            copies[i - near].wait()
        for c in range(2):
            left = jnp.where(row == i, lefts[c], jnp.zeros_like(lefts[c]))
            total += dot(left, block_ref[c], (1, 1))
    total = total[:rows] + total[rows:]
    total_ref[...] = total
    send_ref[...] = total.astype(BF16)


def legendre_kernel(
    nfreq, rows_ref, own_ref, first_ref, second_ref, third_ref, table_ref, out_ref, scratch_ref
):
    total = own_ref[...] + first_ref[...].astype(F32)
    total = total + second_ref[...].astype(F32) + third_ref[...].astype(F32)
    rows = total.shape[0]
    left = jnp.concatenate(split(total), 0)
    row = iota(left.shape, 0) // nfreq
    column = iota(left.shape, 1)
    modes = table_ref.shape[0]
    latitude = jnp.zeros((2 * rows, table_ref.shape[2]), F32)
    for m in range(modes):
        live = (row % modes == m) & (column < rows_ref[m])
        latitude += dot(jnp.where(live, left, jnp.zeros_like(left)), table_ref[m], (1, 0))
    latitude = (latitude[:rows] + latitude[rows:]).T
    scratch_ref[: latitude.shape[0]] = latitude
    dests, _, width = out_ref.shape
    circles = latitude.shape[0] // dests
    pieces = [scratch_ref[pl.ds(j, dests, circles), :] for j in range(circles)]
    out_ref[...] = jnp.concatenate(pieces, 1).reshape(out_ref.shape)


def mode_of(position, modes, mode_dev):
    blocks = modes // mode_dev
    return position % blocks * mode_dev + position // blocks


def table_kernel(modes, mode_dev, count_ref, outer_ref, inner_ref):
    for circle in range(count_ref.shape[0]):
        period = jnp.full((1, 1), 2 * count_ref[circle], jnp.int32).astype(F32)
        inverse = 1.0 / period
        mode = mode_of(iota((OUTER, modes), 1), modes, mode_dev)
        step = iota((OUTER, modes), 0) * (2 * INNER)
        outer_ref[circle, 0], outer_ref[circle, 1] = cos_sin(
            (mode * step).astype(F32), period, inverse
        )
        blocks = modes // mode_dev
        mode = iota((blocks, INNER), 0) * mode_dev
        step = iota((blocks, INNER), 1) * 2 + 1
        cosine, sine = cos_sin((mode * step).astype(F32), period, inverse)
        first = jnp.where(mode == 0, 1.0, 2.0)
        small = (8, INNER)
        small_step = (iota(small, 0) * (iota(small, 1) * 2 + 1)).astype(F32)
        turn_cosine, turn_sine = cos_sin(small_step, period, inverse)
        for j in range(mode_dev):
            c, s = turn_cosine[j : j + 1], turn_sine[j : j + 1]
            factor = first if j == 0 else 2.0
            for part, value in enumerate(
                ((cosine * c - sine * s) * factor, (sine * c + cosine * s) * -factor)
            ):
                high, low = split(value)
                at = part * modes + j * blocks
                inner_ref[circle, at : at + blocks, :INNER] = high
                inner_ref[circle, at : at + blocks, INNER:] = low


def middle_kernel(
    modes, mode_dev, count_ref, after_ref, legendre_ref,
    near_ref, outer_ref, inner_ref, semaphore,
):
    del after_ref
    copy = pltpu.make_async_copy(legendre_ref, near_ref, semaphore)
    copy.start()
    table_kernel(modes, mode_dev, count_ref, outer_ref, inner_ref)
    copy.wait()


def synthesis_kernel(
    nfreq, count_ref, value_ref, outer_ref, inner_ref, out_ref, map_ref, semaphores
):
    circles = outer_ref.shape[0]
    sources, _, width = value_ref.shape
    values = value_ref[...].reshape(sources, width).T
    each = width // circles
    results = []
    for circle in range(circles):
        cosine = outer_ref[circle, 0]
        sine = outer_ref[circle, 1]
        rows = []
        for f in range(nfreq):
            start = circle * each + f
            real, imag = (
                jnp.concatenate([values[i : i + 1] for i in range(at, at + each // 2, nfreq)], 1)
                for at in (start, start + each // 2)
            )
            rows.append(
                jnp.concatenate([real * cosine - imag * sine, real * sine + imag * cosine], 1)
            )
        high, low = split(jnp.concatenate(rows, 0))
        result = dot(jnp.concatenate([high, low], 0), inner_ref[circle], (1, 0))
        half = nfreq * OUTER
        results.append(
            result[:half, :INNER] + (result[:half, INNER:] + result[half:, :INNER])
        )
    pixel = iota((OUTER, INNER), 0) * INNER + iota((OUTER, INNER), 1)
    copies = []
    for f in range(nfreq):
        for circle in range(circles):
            keep = pixel < count_ref[circle]
            part = jnp.where(keep, results[circle][f * OUTER : (f + 1) * OUTER], 0.0)
            for q in range(OUTER):
                map_ref[f, circle : circle + 1, q * INNER : (q + 1) * INNER] = part[q : q + 1]
        copies.append(pltpu.make_async_copy(map_ref.at[f], out_ref.at[f], semaphores.at[f]))
        copies[f].start()
    for copy in copies:
        copy.wait()


def body(visibility, pair_baseline, beam_inverse, block_rows, legendre, circle_pixels):
    ma_count = lax.axis_size("ma")
    freq_count = lax.axis_size("freq")
    time_dev, _, nfreq, base_dev = visibility.shape
    ntime = time_dev * ma_count
    mode_dev, _, _, lrows, _ = beam_inverse.shape
    modes = mode_dev * ma_count
    circles = circle_pixels.shape[0]
    base_half = base_dev // 2
    rows = mode_dev * 2 * nfreq

    other = lax.ppermute(visibility, "ma", [(i, i ^ 1) for i in range(ma_count)])
    table = jnp.asarray(phase_table(modes, mode_dev, nfreq, 2 * time_dev, ntime))
    piece = (time_dev, 2, nfreq, base_half)
    near, left, right = pl.pallas_call(
        fetch_kernel,
        out_shape=(
            pltpu.VMEM(table.shape[1:], BF16),
            pltpu.VMEM(piece, BF16),
            pltpu.VMEM(piece, BF16),
        ),
        in_specs=[ANY, ANY],
        out_specs=(VMEM,) * 3,
        scratch_shapes=[pltpu.SemaphoreType.DMA((3,))],
        compiler_params=PARAMS,
        cost_estimate=pl.CostEstimate(flops=0, bytes_accessed=1200000, transcendentals=0),
        name="fetch",
    )(
        pltpu.with_memory_space_constraint(table, pltpu.HBM),
        pltpu.with_memory_space_constraint(visibility, pltpu.HBM),
    )
    spectrum_shape = (ma_count // 2, rows, base_dev)
    partial_spectrum = pl.pallas_call(
        lambda *refs: time_kernel(nfreq, ma_count // 2, mode_dev, *refs),
        out_shape=jax.ShapeDtypeStruct(spectrum_shape, BF16),
        in_specs=[VMEM] * 5,
        out_specs=ANY,
        scratch_shapes=[pltpu.VMEM(spectrum_shape, BF16), pltpu.SemaphoreType.DMA((4,))],
        compiler_params=PARAMS,
        name="time_sum",
    )(
        *(
            pltpu.with_memory_space_constraint(a, pltpu.VMEM)
            for a in (
                near,
                *(
                    a.reshape(-1, base_half)
                    for a in (left, right, other[..., :base_half], other[..., base_half:])
                ),
            )
        )
    )
    groups = [list(range(core, ma_count, 2)) for core in range(2)]
    received = lax.all_to_all(partial_spectrum, "ma", 0, 0, axis_index_groups=groups)

    blocks = mode_dev * nfreq
    block = beam_inverse.shape[2:]
    far_beam = pltpu.with_memory_space_constraint(beam_inverse, pltpu.HBM)
    weight, *near_blocks = pl.pallas_call(
        lambda *refs: side_kernel(nfreq, *refs),
        out_shape=(pltpu.VMEM((1, base_dev), F32),) + (pltpu.VMEM(block, BF16),) * NEAR,
        in_specs=[VMEM, ANY],
        out_specs=(VMEM,) * (1 + NEAR),
        scratch_shapes=[pltpu.SemaphoreType.DMA((NEAR,))],
        compiler_params=PARAMS,
        cost_estimate=pl.CostEstimate(
            flops=10000000, bytes_accessed=8 * 1024 * 1024, transcendentals=0
        ),
        name="side",
    )(
        pltpu.with_memory_space_constraint(pair_baseline.reshape(-1, 128), pltpu.VMEM),
        far_beam,
    )
    own, send = pl.pallas_call(
        lambda *refs: beam_kernel(nfreq, *refs),
        out_shape=(pltpu.VMEM((rows, lrows), F32), pltpu.VMEM((rows, lrows), BF16)),
        in_specs=[VMEM, VMEM, ANY] + [VMEM] * NEAR,
        out_specs=(VMEM, VMEM),
        scratch_shapes=[
            pltpu.VMEM((blocks - NEAR, *block), BF16),
            pltpu.SemaphoreType.DMA((blocks - NEAR,)),
        ],
        compiler_params=PARAMS,
        name="beam",
    )(
        *(pltpu.with_memory_space_constraint(a, pltpu.VMEM) for a in (received, weight)),
        far_beam,
        *(pltpu.with_memory_space_constraint(a, pltpu.VMEM) for a in near_blocks),
    )
    arrived = [
        lax.ppermute(send, "freq", [(i, (i + k) % freq_count) for i in range(freq_count)])
        for k in range(1, freq_count)
    ]
    near_legendre, outer, inner = pl.pallas_call(
        lambda *refs: middle_kernel(modes, mode_dev, *refs),
        out_shape=(
            pltpu.VMEM(legendre.shape, BF16),
            pltpu.VMEM((circles, 2, OUTER, modes), F32),
            pltpu.VMEM((circles, 2 * modes, 2 * INNER), BF16),
        ),
        in_specs=[SMEM, ANY, ANY],
        out_specs=(VMEM,) * 3,
        scratch_shapes=[pltpu.SemaphoreType.DMA(())],
        compiler_params=PARAMS,
        cost_estimate=pl.CostEstimate(
            flops=10000000, bytes_accessed=4200000, transcendentals=0
        ),
        name="middle",
    )(circle_pixels, own, pltpu.with_memory_space_constraint(legendre, pltpu.HBM))
    latitude = pl.pallas_call(
        lambda *refs: legendre_kernel(nfreq, *refs),
        out_shape=(pltpu.VMEM((ma_count, 1, circles * rows), F32),),
        in_specs=[SMEM] + [VMEM] * 5,
        out_specs=(VMEM,),
        scratch_shapes=[pltpu.VMEM((legendre.shape[2] + 8, rows), F32)],
        compiler_params=PARAMS,
        name="legendre",
    )(
        block_rows,
        *(
            pltpu.with_memory_space_constraint(a, pltpu.VMEM)
            for a in (own, *arrived, near_legendre)
        ),
    )[0]
    regrouped = lax.all_to_all(latitude, "ma", 0, 0)
    return pl.pallas_call(
        lambda *refs: synthesis_kernel(nfreq, *refs),
        out_shape=jax.ShapeDtypeStruct((nfreq, circles, PMAX), F32),
        in_specs=[SMEM, VMEM, VMEM, VMEM],
        out_specs=ANY,
        scratch_shapes=[
            pltpu.VMEM((nfreq, circles, PMAX), F32),
            pltpu.SemaphoreType.DMA((nfreq,)),
        ],
        compiler_params=PARAMS,
        name="synthesis",
    )(
        circle_pixels,
        *(pltpu.with_memory_space_constraint(a, pltpu.VMEM) for a in (regrouped, outer, inner)),
    )


def solution(mesh):
    return jax.shard_map(
        body,
        mesh=mesh,
        in_specs=(
            P("ma", None, None, "freq"),
            P(),
            P("ma", None, None, None, "freq"),
            P("ma"),
            P("ma", None, "freq"),
            P(("freq", "ma")),
        ),
        out_specs=P(None, ("freq", "ma"), None),
        check_vma=False,
    )
```

```python
import math

import jax
import jax.numpy as jnp
import ml_dtypes
import numpy as np
from jax import lax
from jax.experimental import pallas as pl
from jax.experimental.pallas import tpu as pltpu
from jax.sharding import PartitionSpec as P

PMAX = 2048
INNER = 128
OUTER = PMAX // INNER
NEAR = 3
COS = (
    1.0, -19.739208221435547, 64.93939208984375, -85.45664978027344,
    60.24201202392578, -26.403913497924805, 7.797765254974365, -1.4502166509628296,
)
SIN = (
    6.2831854820251465, -41.34170150756836, 81.6052474975586, -76.70579528808594,
    42.057708740234375, -15.086281776428223, 3.7804296016693115, -0.6196905970573425,
)
BF16 = jnp.bfloat16
F32 = jnp.float32
SMEM = pl.BlockSpec(memory_space=pltpu.SMEM)
VMEM = pl.BlockSpec(memory_space=pltpu.VMEM)
ANY = pl.BlockSpec(memory_space=pl.ANY)
PARAMS = pltpu.CompilerParams(vmem_limit_bytes=16 * 1024 * 1024)


def split(x):
    high = x.astype(BF16)
    return high, (x - high.astype(F32)).astype(BF16)


def iota(shape, dimension):
    return lax.broadcasted_iota(jnp.int32, shape, dimension)


def polynomial(square, terms):
    total = jnp.full_like(square, terms[-1])
    for term in terms[-2::-1]:
        total = total * square + term
    return total


def cos_sin(phase, period, inverse):
    rest = phase - jnp.round(phase * inverse) * period
    turn = rest * inverse
    square = turn * turn
    return polynomial(square, COS), polynomial(square, SIN) * turn


def dot(a, b, contract):
    return lax.dot_general(a, b, ((contract[:1], contract[1:]), ((), ())), preferred_element_type=F32)


def call(kernel, outs, specs, *args, name=None):
    args = [
        pltpu.with_memory_space_constraint(a, pltpu.VMEM) if s is VMEM else a
        for a, s in zip(args, specs)
    ]
    return pl.pallas_call(
        kernel,
        out_shape=tuple(pltpu.VMEM(s, d) for s, d in outs),
        in_specs=list(specs),
        out_specs=tuple(VMEM for _ in outs),
        compiler_params=PARAMS,
        name=name,
    )(*args)


def phase_table(modes, mode_dev, nfreq, chip_times, ntime):
    half = modes // 2
    row = np.arange(2 * half * nfreq)[:, None]
    column = np.arange(chip_times * 2 * nfreq)[None, :]
    part_out, place, freq_out = row // (half * nfreq), row // nfreq % half, row % nfreq
    time, part_in, freq_in = column // (2 * nfreq), column // nfreq % 2, column % nfreq
    tables = []
    for core in range(2):
        mode = place // mode_dev * (2 * mode_dev) + core * mode_dev + place % mode_dev
        phase = (mode * time + (part_out - part_in) * (ntime // 4)) % ntime
        value = np.cos(phase * (2.0 * math.pi / ntime)) / math.sqrt(ntime)
        value = value * (freq_out == freq_in)
        high = value.astype(ml_dtypes.bfloat16)
        low = (value - high.astype(np.float64)).astype(ml_dtypes.bfloat16)
        tables.append(np.stack([high, low]))
    return np.stack(tables)


def fetch_kernel(table_ref, signal_ref, near_ref, left_ref, right_ref, semaphores):
    width = left_ref.shape[3]
    copies = [
        pltpu.make_async_copy(
            signal_ref.at[:, :, :, :width], left_ref, semaphores.at[0]
        ),
        pltpu.make_async_copy(
            signal_ref.at[:, :, :, width:], right_ref, semaphores.at[1]
        ),
        pltpu.make_async_copy(
            table_ref.at[lax.rem(lax.axis_index("ma"), 2)], near_ref, semaphores.at[2]
        ),
    ]
    for copy in copies:
        copy.start()
    for copy in copies:
        copy.wait()


def time_kernel(nfreq, chips, mode_dev, table_ref, *refs):
    *signal_refs, out_ref = refs
    place = lax.axis_index("ma")
    core = lax.rem(place, 2)
    own_left, own_right, other_left, other_right = (ref[...] for ref in signal_refs)
    own = jnp.concatenate([own_left, own_right], 1)
    other = jnp.concatenate([other_left, other_right], 1)
    even = core == 0
    signal = jnp.concatenate([jnp.where(even, own, other), jnp.where(even, other, own)], 0)
    total = dot(table_ref[0], signal, (1, 0)) + dot(table_ref[1], signal, (1, 0))
    dests, rows, width = out_ref.shape
    period = chips // 2 * nfreq
    index = iota((period, width), 0) // nfreq
    mode = index // mode_dev * (2 * mode_dev) + core * mode_dev + index % mode_dev
    phase = mode * lax.div(place, 2)
    turn = ((phase + chips // 2) % chips - chips // 2).astype(F32) * (1.0 / chips)
    square = turn * turn
    cosine, sine = polynomial(square, COS)[None], (polynomial(square, SIN) * turn)[None]
    real, imag = total.reshape(2, -1, period, width)
    shape = (dests, rows // 2, width)
    real, imag = real * cosine + imag * sine, imag * cosine - real * sine
    out_ref[...] = jnp.concatenate([real.reshape(shape), imag.reshape(shape)], 1).astype(BF16)


def side_kernel(nfreq, pair_ref, beam_ref, weight_ref, *refs):
    *block_refs, semaphores = refs
    copies = fetch_blocks(nfreq, beam_ref, 0, block_refs, semaphores)
    shape = (weight_ref.shape[1], pair_ref.shape[1])
    ids = iota(shape, 0) + lax.axis_index("freq") * shape[0]
    total = jnp.zeros(shape, F32)
    for i in range(pair_ref.shape[0]):
        total += jnp.where(pair_ref[i : i + 1, :] == ids, 1.0, 0.0)
    weight_ref[...] = jnp.sqrt(jnp.sum(total.T, 0, keepdims=True))
    for copy in copies:
        copy.wait()


def fetch_blocks(nfreq, beam_ref, first, block_refs, semaphores):
    copies = [
        pltpu.make_async_copy(
            beam_ref.at[(first + i) // nfreq, (first + i) % nfreq], block_ref, semaphores.at[i]
        )
        for i, block_ref in enumerate(block_refs)
    ]
    for copy in copies:
        copy.start()
    return copies


def beam_kernel(nfreq, part_ref, weight_ref, beam_ref, *refs):
    *near_refs, total_ref, send_ref, far_ref, semaphores = refs
    near = len(near_refs)
    far_refs = [far_ref.at[i] for i in range(far_ref.shape[0])]
    copies = fetch_blocks(nfreq, beam_ref, near, far_refs, semaphores)
    rows = part_ref.shape[1]
    half = rows // 2
    weighted = part_ref[...].astype(F32).sum(0) * weight_ref[...]
    turned = jnp.concatenate([-weighted[half:], weighted[:half]], 0)
    row = iota((2 * rows, weighted.shape[1]), 0) % half
    lefts = [jnp.concatenate(split(value), 0) for value in (weighted, turned)]
    total = jnp.zeros((2 * rows, total_ref.shape[1]), F32)
    for i, block_ref in enumerate([*near_refs, *far_refs]):
        if i >= near:
            copies[i - near].wait()
        for c in range(2):
            left = jnp.where(row == i, lefts[c], jnp.zeros_like(lefts[c]))
            total += dot(left, block_ref[c], (1, 1))
    total = total[:rows] + total[rows:]
    total_ref[...] = total
    send_ref[...] = total.astype(BF16)


def legendre_kernel(
    nfreq, rows_ref, own_ref, first_ref, second_ref, third_ref, table_ref, out_ref, scratch_ref
):
    total = own_ref[...] + first_ref[...].astype(F32)
    total = total + second_ref[...].astype(F32) + third_ref[...].astype(F32)
    rows = total.shape[0]
    left = jnp.concatenate(split(total), 0)
    row = iota(left.shape, 0) // nfreq
    column = iota(left.shape, 1)
    modes = table_ref.shape[0]
    latitude = jnp.zeros((2 * rows, table_ref.shape[2]), F32)
    for m in range(modes):
        live = (row % modes == m) & (column < rows_ref[m])
        latitude += dot(jnp.where(live, left, jnp.zeros_like(left)), table_ref[m], (1, 0))
    latitude = (latitude[:rows] + latitude[rows:]).T
    scratch_ref[: latitude.shape[0]] = latitude
    dests, _, width = out_ref.shape
    circles = latitude.shape[0] // dests
    pieces = [scratch_ref[pl.ds(j, dests, circles), :] for j in range(circles)]
    out_ref[...] = jnp.concatenate(pieces, 1).reshape(out_ref.shape)


def mode_of(position, modes, mode_dev):
    blocks = modes // mode_dev
    return position % blocks * mode_dev + position // blocks


def table_kernel(modes, mode_dev, count_ref, outer_ref, inner_ref):
    for circle in range(count_ref.shape[0]):
        period = jnp.full((1, 1), 2 * count_ref[circle], jnp.int32).astype(F32)
        inverse = 1.0 / period
        mode = mode_of(iota((OUTER, modes), 1), modes, mode_dev)
        step = iota((OUTER, modes), 0) * (2 * INNER)
        outer_ref[circle, 0], outer_ref[circle, 1] = cos_sin(
            (mode * step).astype(F32), period, inverse
        )
        blocks = modes // mode_dev
        mode = iota((blocks, INNER), 0) * mode_dev
        step = iota((blocks, INNER), 1) * 2 + 1
        cosine, sine = cos_sin((mode * step).astype(F32), period, inverse)
        first = jnp.where(mode == 0, 1.0, 2.0)
        small = (8, INNER)
        small_step = (iota(small, 0) * (iota(small, 1) * 2 + 1)).astype(F32)
        turn_cosine, turn_sine = cos_sin(small_step, period, inverse)
        for j in range(mode_dev):
            c, s = turn_cosine[j : j + 1], turn_sine[j : j + 1]
            factor = first if j == 0 else 2.0
            for part, value in enumerate(
                ((cosine * c - sine * s) * factor, (sine * c + cosine * s) * -factor)
            ):
                high, low = split(value)
                at = part * modes + j * blocks
                inner_ref[circle, at : at + blocks, :INNER] = high
                inner_ref[circle, at : at + blocks, INNER:] = low


def middle_kernel(
    modes, mode_dev, count_ref, after_ref, legendre_ref,
    near_ref, outer_ref, inner_ref, semaphores,
):
    del after_ref
    copies = [
        pltpu.make_async_copy(legendre_ref.at[m], near_ref.at[m], semaphores.at[m])
        for m in range(near_ref.shape[0])
    ]
    for copy in copies:
        copy.start()
    table_kernel(modes, mode_dev, count_ref, outer_ref, inner_ref)
    for copy in copies:
        copy.wait()


def synthesis_kernel(nfreq, count_ref, value_ref, outer_ref, inner_ref, map_ref):
    circles = outer_ref.shape[0]
    sources, _, width = value_ref.shape
    values = value_ref[...].reshape(sources, width).T
    each = width // circles
    results = []
    for circle in range(circles):
        cosine = outer_ref[circle, 0]
        sine = outer_ref[circle, 1]
        rows = []
        for f in range(nfreq):
            start = circle * each + f
            real, imag = (
                jnp.concatenate([values[i : i + 1] for i in range(at, at + each // 2, nfreq)], 1)
                for at in (start, start + each // 2)
            )
            rows.append(
                jnp.concatenate([real * cosine - imag * sine, real * sine + imag * cosine], 1)
            )
        high, low = split(jnp.concatenate(rows, 0))
        result = dot(jnp.concatenate([high, low], 0), inner_ref[circle], (1, 0))
        half = nfreq * OUTER
        results.append(
            result[:half, :INNER] + (result[:half, INNER:] + result[half:, :INNER])
        )
    pixel = iota((OUTER, INNER), 0) * INNER + iota((OUTER, INNER), 1)
    for circle in range(circles):
        keep = pixel < count_ref[circle]
        for f in range(nfreq):
            part = jnp.where(keep, results[circle][f * OUTER : (f + 1) * OUTER], 0.0)
            for q in range(OUTER):
                map_ref[f, circle : circle + 1, q * INNER : (q + 1) * INNER] = part[q : q + 1]


def body(visibility, pair_baseline, beam_inverse, block_rows, legendre, circle_pixels):
    ma_count = lax.axis_size("ma")
    freq_count = lax.axis_size("freq")
    time_dev, _, nfreq, base_dev = visibility.shape
    ntime = time_dev * ma_count
    mode_dev, _, _, lrows, _ = beam_inverse.shape
    modes = mode_dev * ma_count
    circles = circle_pixels.shape[0]
    base_half = base_dev // 2
    rows = mode_dev * 2 * nfreq

    other = lax.ppermute(visibility, "ma", [(i, i ^ 1) for i in range(ma_count)])
    table = jnp.asarray(phase_table(modes, mode_dev, nfreq, 2 * time_dev, ntime))
    piece = (time_dev, 2, nfreq, base_half)
    near, left, right = pl.pallas_call(
        fetch_kernel,
        out_shape=(
            pltpu.VMEM(table.shape[1:], BF16),
            pltpu.VMEM(piece, BF16),
            pltpu.VMEM(piece, BF16),
        ),
        in_specs=[ANY, ANY],
        out_specs=(VMEM,) * 3,
        scratch_shapes=[pltpu.SemaphoreType.DMA((3,))],
        compiler_params=PARAMS,
        cost_estimate=pl.CostEstimate(flops=0, bytes_accessed=1200000, transcendentals=0),
        name="fetch",
    )(
        pltpu.with_memory_space_constraint(table, pltpu.HBM),
        pltpu.with_memory_space_constraint(visibility, pltpu.HBM),
    )
    (partial_spectrum,) = call(
        lambda *refs: time_kernel(nfreq, ma_count // 2, mode_dev, *refs),
        [((ma_count // 2, rows, base_dev), BF16)],
        [VMEM] * 5,
        near,
        *(
            a.reshape(-1, base_half)
            for a in (left, right, other[..., :base_half], other[..., base_half:])
        ),
        name="time_sum",
    )
    groups = [list(range(core, ma_count, 2)) for core in range(2)]
    received = lax.all_to_all(partial_spectrum, "ma", 0, 0, axis_index_groups=groups)

    blocks = mode_dev * nfreq
    block = beam_inverse.shape[2:]
    far_beam = pltpu.with_memory_space_constraint(beam_inverse, pltpu.HBM)
    weight, *near_blocks = pl.pallas_call(
        lambda *refs: side_kernel(nfreq, *refs),
        out_shape=(pltpu.VMEM((1, base_dev), F32),) + (pltpu.VMEM(block, BF16),) * NEAR,
        in_specs=[VMEM, ANY],
        out_specs=(VMEM,) * (1 + NEAR),
        scratch_shapes=[pltpu.SemaphoreType.DMA((NEAR,))],
        compiler_params=PARAMS,
        cost_estimate=pl.CostEstimate(
            flops=10000000, bytes_accessed=8 * 1024 * 1024, transcendentals=0
        ),
        name="side",
    )(
        pltpu.with_memory_space_constraint(pair_baseline.reshape(-1, 128), pltpu.VMEM),
        far_beam,
    )
    own, send = pl.pallas_call(
        lambda *refs: beam_kernel(nfreq, *refs),
        out_shape=(pltpu.VMEM((rows, lrows), F32), pltpu.VMEM((rows, lrows), BF16)),
        in_specs=[VMEM, VMEM, ANY] + [VMEM] * NEAR,
        out_specs=(VMEM, VMEM),
        scratch_shapes=[
            pltpu.VMEM((blocks - NEAR, *block), BF16),
            pltpu.SemaphoreType.DMA((blocks - NEAR,)),
        ],
        compiler_params=PARAMS,
        name="beam",
    )(
        *(pltpu.with_memory_space_constraint(a, pltpu.VMEM) for a in (received, weight)),
        far_beam,
        *(pltpu.with_memory_space_constraint(a, pltpu.VMEM) for a in near_blocks),
    )
    arrived = [
        lax.ppermute(send, "freq", [(i, (i + k) % freq_count) for i in range(freq_count)])
        for k in range(1, freq_count)
    ]
    near_legendre, outer, inner = pl.pallas_call(
        lambda *refs: middle_kernel(modes, mode_dev, *refs),
        out_shape=(
            pltpu.VMEM(legendre.shape, BF16),
            pltpu.VMEM((circles, 2, OUTER, modes), F32),
            pltpu.VMEM((circles, 2 * modes, 2 * INNER), BF16),
        ),
        in_specs=[SMEM, ANY, ANY],
        out_specs=(VMEM,) * 3,
        scratch_shapes=[pltpu.SemaphoreType.DMA((mode_dev,))],
        compiler_params=PARAMS,
        cost_estimate=pl.CostEstimate(
            flops=10000000, bytes_accessed=4200000, transcendentals=0
        ),
        name="middle",
    )(circle_pixels, own, pltpu.with_memory_space_constraint(legendre, pltpu.HBM))
    latitude = pl.pallas_call(
        lambda *refs: legendre_kernel(nfreq, *refs),
        out_shape=(pltpu.VMEM((ma_count, 1, circles * rows), F32),),
        in_specs=[SMEM] + [VMEM] * 5,
        out_specs=(VMEM,),
        scratch_shapes=[pltpu.VMEM((legendre.shape[2] + 8, rows), F32)],
        compiler_params=PARAMS,
        name="legendre",
    )(
        block_rows,
        *(
            pltpu.with_memory_space_constraint(a, pltpu.VMEM)
            for a in (own, *arrived, near_legendre)
        ),
    )[0]
    regrouped = lax.all_to_all(latitude, "ma", 0, 0)
    return pl.pallas_call(
        lambda *refs: synthesis_kernel(nfreq, *refs),
        out_shape=jax.ShapeDtypeStruct((nfreq, circles, PMAX), F32),
        in_specs=[SMEM, VMEM, VMEM, VMEM],
        out_specs=VMEM,
        compiler_params=PARAMS,
        name="synthesis",
    )(
        circle_pixels,
        *(pltpu.with_memory_space_constraint(a, pltpu.VMEM) for a in (regrouped, outer, inner)),
    )


def solution(mesh):
    return jax.shard_map(
        body,
        mesh=mesh,
        in_specs=(
            P("ma", None, None, "freq"),
            P(),
            P("ma", None, None, None, "freq"),
            P("ma"),
            P("ma", None, "freq"),
            P(("freq", "ma")),
        ),
        out_specs=P(None, ("freq", "ma"), None),
        check_vma=False,
    )
```
